32 devices in a mesh: stn: 8 (over z, x), beam: 4 (over y, core).
Axes of the slice: x: 2, y: 2, z: 4, core: 2. Of those that a mesh axis runs over, the one named last changes fastest.
Arguments:
- voltages: bfloat16 [64, 2, 614400], P(('stn', 'beam')), may hold values from -6 to 6
- fir_taps: float32 [12, 8192], replicated, may hold values from -1.75 to 1.75
- delays: float32 [8, 64, 64], P('stn', 'beam'), may hold values from -16 to 16
- taper: float32 [64, 64], replicated, may hold values from 0.5 to 2
- station_map: int32 [64], replicated, may hold values from 0 to 63, each once
- beam_order: int32 [64], replicated, may hold values from 0 to 63, each once
- owners: int32 [4], replicated, may hold values from 0 to 7
Outputs:
- beams_re: float32 [64, 4096, 128], P('beam', 'stn')
- beams_im: float32 [64, 4096, 128], P('beam', 'stn')
The draws below stay inside these ranges and needn't reach their ends.
Inputs may be any that keep to these rules, and one draw needn't show every extreme that they name: `station_map`: each station row holds a different physical station. `beam_order`: each beam slot forms a different beam.
All inputs are finite; a program needn't handle non-finite values.
Results may differ from the reference program's by a relative error of at most 0.0064.
Values may be sent and summed in bfloat16 or wider, within the bound.
A program may use at most 128 MiB of HBM per device.

```python
import math
import jax
import jax.numpy as jnp
from jax import lax

P_SIZE = 64
Q = 128
TAPS = 12
POL = 2
BEAMS = 64
FRAMES = 64
NFFT = 8192
CHANNELS = 4096
CH_DEV = 512
STATIONS = 64
BEAMS_G = 16
GROUPS = 4
OWNERS = 8
N_STN = 8


def place_ends(drawn, own_key, smallest, largest):
    longest = drawn.shape.index(max(drawn.shape))
    spots = []
    for shift in (0, 1):
        where = [jax.random.randint(jax.random.fold_in(own_key, axis), (), 0, length) for axis, length in enumerate(drawn.shape)]
        where[longest] = (where[longest] + shift) % drawn.shape[longest]
        spots.append(tuple(where))
    return drawn.at[spots[0]].set(smallest).at[spots[1]].set(largest)


def levels(own_key, dims, pieces, smallest, high):
    level, own = 1.0, jax.random.fold_in(own_key, 6)
    for axis_at, blocks in pieces:
        steps = jnp.exp(jax.random.uniform(jax.random.fold_in(own, axis_at), (blocks,), jnp.float32, smallest / len(pieces), high / len(pieces)))
        level = level * jnp.repeat(steps, dims[axis_at] // blocks).reshape([-1 if axis == axis_at else 1 for axis in range(len(dims))])
    return level


def scatter_about(rng, dims, width, limit, pieces=(), kind=jnp.bfloat16):
    values = width * jax.random.normal(rng, dims, jnp.float32)
    if pieces:
        values = values * levels(rng, dims, pieces, -0.22, 0.18)
    return jnp.clip(values, -limit, limit).astype(kind)


def setup_inputs(seed: int = 0) -> dict:
    arg_keys = jax.random.split(jax.random.key(seed), 8)
    return {
        "voltages": scatter_about(arg_keys[0], (STATIONS, POL, (FRAMES + TAPS - 1) * NFFT), 1.0, 6.0, ((0, 32),)),
        "fir_taps": scatter_about(arg_keys[1], (TAPS, NFFT), TAPS ** -0.5, 1.75, (), jnp.float32),
        "delays": jnp.clip(jax.random.uniform(arg_keys[2], (OWNERS, BEAMS, STATIONS), jnp.float32, -16.0, 16.0) * levels(arg_keys[2], (OWNERS, BEAMS, STATIONS), ((0, 8), (1, 4)), -0.4, 0.0), -16.0, 16.0),
        "taper": jnp.clip(jnp.exp(jax.random.uniform(arg_keys[3], (BEAMS, STATIONS), jnp.float32, math.log(0.5), math.log(2.0))), 0.5, 2.0),
        "station_map": jax.random.permutation(arg_keys[4], STATIONS).astype(jnp.int32),
        "beam_order": jax.random.permutation(arg_keys[5], BEAMS).astype(jnp.int32),
        "owners": place_ends(jax.random.randint(arg_keys[6], (GROUPS,), 0, OWNERS), jax.random.fold_in(arg_keys[6], 1), 0, OWNERS - 1).astype(jnp.int32),
    }


TWO_PI = 2.0 * math.pi

def dft_tables():
    first_idx = jnp.arange(P_SIZE, dtype=jnp.int32)
    second_idx = jnp.arange(Q, dtype=jnp.int32)
    half_idx = jnp.arange(Q // 2, dtype=jnp.int32)
    first_angle = TWO_PI / P_SIZE * (first_idx[:, None] * first_idx[None, :] % P_SIZE).astype(jnp.float32)
    twist_angle = TWO_PI / (P_SIZE * Q) * (first_idx[:, None] * second_idx[None, :]).astype(jnp.float32)
    second_angle = TWO_PI / Q * (second_idx[:, None] * half_idx[None, :] % Q).astype(jnp.float32)
    return (jnp.cos(first_angle).astype(jnp.bfloat16), jnp.sin(first_angle).astype(jnp.bfloat16), jnp.cos(twist_angle), jnp.sin(twist_angle), jnp.cos(second_angle).astype(jnp.bfloat16), jnp.sin(second_angle).astype(jnp.bfloat16))

def beam_weights(delay_cols, gain_cols, chan_ids):
    phase = delay_cols[:, :, None] * chan_ids.astype(jnp.float32)[None, None, :] * (TWO_PI / (P_SIZE * Q))
    weight_re = (gain_cols[:, :, None] * jnp.cos(phase)).astype(jnp.bfloat16)
    weight_im = (-(gain_cols[:, :, None] * jnp.sin(phase))).astype(jnp.bfloat16)
    return (weight_re, weight_im)

def channelize(samples, fir_taps, tables):
    cos_one, sin_one, twist_cos, twist_sin, cos_two, sin_two = tables
    blocks = samples.reshape(POL, FRAMES + TAPS - 1, P_SIZE * Q).astype(jnp.float32)
    filtered = jnp.zeros((POL, FRAMES, P_SIZE * Q), jnp.float32)
    for tap_idx in range(TAPS):
        filtered = filtered + fir_taps[tap_idx] * blocks[:, tap_idx:tap_idx + FRAMES]
    folded = lax.optimization_barrier(filtered.astype(jnp.bfloat16))
    folded = folded.astype(jnp.float32).reshape(POL, FRAMES, P_SIZE, Q)
    first_re = jnp.einsum('pfnq,an->pfaq', folded, cos_one.astype(jnp.float32))
    first_im = -jnp.einsum('pfnq,an->pfaq', folded, sin_one.astype(jnp.float32))
    turned_re = (first_re * twist_cos + first_im * twist_sin).astype(jnp.bfloat16)
    turned_im = (first_im * twist_cos - first_re * twist_sin).astype(jnp.bfloat16)
    turned_re, turned_im = lax.optimization_barrier((turned_re, turned_im))
    turned_re = turned_re.astype(jnp.float32)
    turned_im = turned_im.astype(jnp.float32)
    cos_wide = cos_two.astype(jnp.float32)
    sin_wide = sin_two.astype(jnp.float32)
    chan_re = jnp.einsum('pfaq,qb->bapf', turned_re, cos_wide) + jnp.einsum('pfaq,qb->bapf', turned_im, sin_wide)
    chan_im = jnp.einsum('pfaq,qb->bapf', turned_im, cos_wide) - jnp.einsum('pfaq,qb->bapf', turned_re, sin_wide)
    return (chan_re.astype(jnp.bfloat16).reshape(CHANNELS, POL * FRAMES), chan_im.astype(jnp.bfloat16).reshape(CHANNELS, POL * FRAMES))

def reference(voltages, fir_taps, delays, taper, station_map, beam_order, owners):
    tables = dft_tables()
    chan_re, chan_im = lax.map(lambda samples: channelize(samples, fir_taps, tables), voltages)
    slot_ids = jnp.arange(BEAMS, dtype=jnp.int32)
    slot_owner = owners[slot_ids // BEAMS_G]
    slot_delay = delays[slot_owner, slot_ids]
    delay_rows = slot_delay[:, station_map]
    gain_rows = taper[beam_order][:, station_map]
    beam_scale = 1.0 / math.sqrt(P_SIZE * Q * STATIONS)

    def one_block(block_idx):
        first_chan = block_idx * CH_DEV
        part_re = lax.dynamic_slice_in_dim(chan_re, first_chan, CH_DEV, 1).astype(jnp.float32)
        part_im = lax.dynamic_slice_in_dim(chan_im, first_chan, CH_DEV, 1).astype(jnp.float32)
        chan_ids = first_chan + jnp.arange(CH_DEV, dtype=jnp.int32)
        weight_re, weight_im = beam_weights(delay_rows, gain_rows, chan_ids)
        weight_re = weight_re.astype(jnp.float32)
        weight_im = weight_im.astype(jnp.float32)
        beam_re = (jnp.einsum('jrk,rkc->jkc', weight_re, part_re) - jnp.einsum('jrk,rkc->jkc', weight_im, part_im)) * beam_scale
        beam_im = (jnp.einsum('jrk,rkc->jkc', weight_re, part_im) + jnp.einsum('jrk,rkc->jkc', weight_im, part_re)) * beam_scale
        return (beam_re, beam_im)
    block_re, block_im = lax.map(one_block, jnp.arange(N_STN, dtype=jnp.int32))
    beams_re = jnp.transpose(block_re, (1, 0, 2, 3)).reshape(BEAMS, CHANNELS, POL * FRAMES)
    beams_im = jnp.transpose(block_im, (1, 0, 2, 3)).reshape(BEAMS, CHANNELS, POL * FRAMES)
    return (beams_re, beams_im)
```

```python
import functools
import math

import jax
import jax.numpy as jnp
from jax import lax
from jax.experimental import pallas as pl
from jax.experimental.pallas import tpu as pltpu
from jax.sharding import PartitionSpec as P

P_SIZE = 64
Q = 128
CHANNELS = 4096
NFFT = P_SIZE * Q
TILE_B = 8
TWO_PI = 2.0 * math.pi
VMEM_LIMIT = 56 * 1024 * 1024

SIN_COEF = (6.283185272447949, -41.34169703819964, 81.60502363802586, -76.70153767014536, 42.01607576124393, -14.86832274947347, 3.199338841413777)
COS_COEF = (0.999999999885554, -19.739208743453883, 64.93938907589225, -85.45665831478402, 60.242131338256826, -26.404668186962848, 7.800131436606334, -1.4531123148805878)


def sin_cos_turns(turns):
    u = turns - jnp.round(turns)
    w = u * u
    s = jnp.full_like(u, SIN_COEF[-1])
    for coef in SIN_COEF[-2::-1]:
        s = s * w + coef
    c = jnp.full_like(u, COS_COEF[-1])
    for coef in COS_COEF[-2::-1]:
        c = c * w + coef
    return s * u, c


def dft_tables():
    first_idx = jnp.arange(P_SIZE, dtype=jnp.int32)
    second_idx = jnp.arange(Q, dtype=jnp.int32)
    half_idx = jnp.arange(Q // 2, dtype=jnp.int32)
    first_angle = (
        TWO_PI / P_SIZE * (first_idx[:, None] * first_idx[None, :] % P_SIZE).astype(jnp.float32)
    )
    twist_angle = (
        TWO_PI / (P_SIZE * Q) * (first_idx[:, None] * second_idx[None, :]).astype(jnp.float32)
    )
    second_angle = TWO_PI / Q * (second_idx[:, None] * half_idx[None, :] % Q).astype(jnp.float32)
    first = jnp.concatenate((jnp.cos(first_angle), -jnp.sin(first_angle)), axis=0)
    cos_two = jnp.cos(second_angle).T.reshape(-1, TILE_B, Q)
    sin_two = jnp.sin(second_angle).T.reshape(-1, TILE_B, Q)
    re_rows = jnp.concatenate((cos_two, sin_two), axis=2)
    im_rows = jnp.concatenate((-sin_two, cos_two), axis=2)
    second = jnp.stack((re_rows, im_rows), axis=1).reshape(Q, 2 * Q)
    return (
        first.astype(jnp.bfloat16),
        jnp.cos(twist_angle),
        jnp.sin(twist_angle),
        second.astype(jnp.bfloat16),
    )


def filter_station(volt_ref, taps_ref, filt, pols, frames, tap_count):
    group = 8
    for part in range(P_SIZE // 16):
        rows = pl.ds(part * 16, 16)
        taps = [taps_ref[m, rows, :] for m in range(tap_count)]

        def body(idx, carry):
            pol, first = idx // (frames // group), idx % (frames // group) * group
            sums = [None] * group
            for step in range(group + tap_count - 1):
                value = volt_ref[pol, first + step, rows, :].astype(jnp.float32)
                for f in range(group):
                    m = step - f
                    if 0 <= m < tap_count:
                        term = taps[m] * value
                        sums[f] = term if sums[f] is None else sums[f] + term
            for f in range(group):
                filt[pol * frames + first + f, rows, :] = sums[f].astype(jnp.bfloat16)
            return carry

        lax.fori_loop(0, pols * frames // group, body, 0)


def first_section(filt, first_ref, cos_ref, sin_ref, turn_re, turn_im, count):
    table = first_ref[...]
    width = 2

    def body(idx, carry):
        c0 = idx * width
        pair = jnp.concatenate([filt[c0 + i] for i in range(width)], axis=1)
        both = jnp.dot(table, pair, preferred_element_type=jnp.float32)
        for i in range(width):
            re = both[:P_SIZE, i * Q : (i + 1) * Q]
            im = both[P_SIZE:, i * Q : (i + 1) * Q]
            rows = pl.ds(pl.multiple_of((c0 + i) * P_SIZE, P_SIZE), P_SIZE)
            turn_re[rows, :] = re * cos_ref[...] + im * sin_ref[...]
            turn_im[rows, :] = im * cos_ref[...] - re * sin_ref[...]
        return carry

    lax.fori_loop(0, count // width, body, 0, unroll=2)


def second_section(second_ref, turn_re, turn_im, count, store):
    table = second_ref[...]

    def body(a, carry):
        rows = pl.ds(a, count, stride=P_SIZE)
        turned = jnp.concatenate(
            (turn_re[rows, :].astype(jnp.bfloat16), turn_im[rows, :].astype(jnp.bfloat16)), axis=1
        )
        out = lax.dot_general(
            table, turned, (((1,), (1,)), ((), ())), preferred_element_type=jnp.float32
        )
        store(a, out.astype(jnp.bfloat16))
        return carry

    lax.fori_loop(0, P_SIZE, body, 0, unroll=4)


def channel_kernel(
    frames, volt_ref, taps_ref, first_ref, cos_ref, sin_ref, second_ref, out_ref, filt, turn_re, turn_im
):
    pols = volt_ref.shape[1]
    count = pols * frames
    filter_station(volt_ref.at[0], taps_ref, filt, pols, frames, taps_ref.shape[0])
    first_section(filt, first_ref, cos_ref, sin_ref, turn_re, turn_im, count)

    def store(a, value):
        out_ref[:, 0, a] = value.reshape(out_ref.shape[0], 2 * TILE_B, count)

    second_section(second_ref, turn_re, turn_im, count, store)


def channelize(voltages, fir_taps, tables):
    stations, pols, samples = voltages.shape
    tap_count = fir_taps.shape[0]
    blocks = samples // NFFT
    frames = blocks - tap_count + 1
    count = pols * frames
    tiles = P_SIZE // TILE_B
    volts = voltages.reshape(stations, pols, blocks, P_SIZE, Q)
    taps = fir_taps.reshape(tap_count, P_SIZE, Q)
    whole = lambda shape: pl.BlockSpec(shape, lambda l: (0,) * len(shape))
    return pl.pallas_call(
        functools.partial(channel_kernel, frames),
        grid=(stations,),
        in_specs=[
            pl.BlockSpec((1, pols, blocks, P_SIZE, Q), lambda l: (l, 0, 0, 0, 0)),
            whole(taps.shape),
        ]
        + [whole(t.shape) for t in tables],
        out_specs=pl.BlockSpec(
            (tiles, 1, P_SIZE, 2 * TILE_B, count), lambda l: (0, l, 0, 0, 0)
        ),
        out_shape=jax.ShapeDtypeStruct((tiles, stations, P_SIZE, 2 * TILE_B, count), jnp.bfloat16),
        scratch_shapes=[
            pltpu.VMEM((count, P_SIZE, Q), jnp.bfloat16),
            pltpu.VMEM((count * P_SIZE, Q), jnp.float32),
            pltpu.VMEM((count * P_SIZE, Q), jnp.float32),
        ],
        compiler_params=pltpu.CompilerParams(vmem_limit_bytes=VMEM_LIMIT),
        name="channelize",
    )(volts, taps, *tables)


def beam_kernel(step_a, scale, data_ref, delay_ref, gain_ref, base_ref, re_ref, im_ref):
    beams, lanes = delay_ref.shape
    count = data_ref.shape[-1]
    lane = lax.broadcasted_iota(jnp.int32, (TILE_B, lanes), 1)
    row = lax.broadcasted_iota(jnp.int32, (TILE_B, lanes), 0)
    keep = lane % TILE_B == row
    quarter = (lane[:1] // TILE_B % 2).astype(jnp.float32) * 0.25
    delay = delay_ref[...]
    chan = base_ref[...] + (pl.program_id(0) * step_a).astype(jnp.float32)
    sin_t, cos_t = sin_cos_turns(delay * chan * (1.0 / NFFT) - quarter)
    sin_d, cos_d = sin_cos_turns(delay * (1.0 / NFFT))
    part_re = gain_ref[...] * cos_t
    part_im = -(gain_ref[...] * sin_t)

    def spread(part):
        return (
            jnp.where(keep[None], part[:, None, :], 0.0)
            .astype(jnp.bfloat16)
            .reshape(beams * TILE_B, lanes)
        )

    out_re = re_ref.reshape(beams * TILE_B * step_a, count)
    out_im = im_ref.reshape(beams * TILE_B * step_a, count)
    for a in range(step_a):
        if a:
            part_re, part_im = (
                part_re * cos_d + part_im * sin_d,
                part_im * cos_d - part_re * sin_d,
            )
        data = data_ref[:, a].reshape(lanes, count)
        rows = pl.ds(a, beams * TILE_B, stride=step_a)
        out_re[rows, :] = (
            jnp.dot(spread(part_re), data, preferred_element_type=jnp.float32) * scale
        )
        out_im[rows, :] = (
            jnp.dot(spread(part_im), data, preferred_element_type=jnp.float32) * scale
        )


def form_beams(data, delay, gain, first_chan, scale):
    stations, _, tile_rows, count = data.shape
    beams = delay.shape[0]
    lanes = stations * tile_rows
    step_a = 8
    base = first_chan + P_SIZE * (jnp.arange(lanes, dtype=jnp.int32) % TILE_B)
    spec = lambda shape: pl.BlockSpec(shape, lambda i: (0,) * len(shape))
    out_spec = pl.BlockSpec((beams * TILE_B, step_a, count), lambda i: (0, i, 0))
    out_shape = jax.ShapeDtypeStruct((beams * TILE_B, P_SIZE, count), jnp.float32)
    re, im = pl.pallas_call(
        functools.partial(beam_kernel, step_a, scale),
        grid=(P_SIZE // step_a,),
        in_specs=[
            pl.BlockSpec((stations, step_a, tile_rows, count), lambda i: (0, i, 0, 0)),
            spec((beams, lanes)),
            spec((beams, lanes)),
            spec((1, lanes)),
        ],
        out_specs=[out_spec, out_spec],
        out_shape=[out_shape, out_shape],
        compiler_params=pltpu.CompilerParams(vmem_limit_bytes=VMEM_LIMIT),
        name="form_beams",
    )(
        data,
        jnp.repeat(delay, tile_rows, axis=1),
        jnp.repeat(gain, tile_rows, axis=1),
        base.astype(jnp.float32)[None],
    )
    shape = (beams, TILE_B * P_SIZE, count)
    return re.reshape(shape), im.reshape(shape)


def from_root(value, axis, source):
    kept = jnp.where(lax.axis_index(axis) == source, value, 0).astype(value.dtype)
    return lax.psum(kept, axis)


def general_tables():
    first_idx = jnp.arange(P_SIZE, dtype=jnp.int32)
    second_idx = jnp.arange(Q, dtype=jnp.int32)
    half_idx = jnp.arange(Q // 2, dtype=jnp.int32)
    first_angle = (
        TWO_PI / P_SIZE * (first_idx[:, None] * first_idx[None, :] % P_SIZE).astype(jnp.float32)
    )
    twist_angle = (
        TWO_PI / (P_SIZE * Q) * (first_idx[:, None] * second_idx[None, :]).astype(jnp.float32)
    )
    second_angle = TWO_PI / Q * (second_idx[:, None] * half_idx[None, :] % Q).astype(jnp.float32)
    return (
        jnp.cos(first_angle).astype(jnp.bfloat16),
        jnp.sin(first_angle).astype(jnp.bfloat16),
        jnp.cos(twist_angle),
        jnp.sin(twist_angle),
        jnp.cos(second_angle).astype(jnp.bfloat16),
        jnp.sin(second_angle).astype(jnp.bfloat16),
    )


def beam_weights(delay_cols, gain_cols, chan_ids):
    phase = (
        delay_cols[:, :, None]
        * chan_ids.astype(jnp.float32)[None, None, :]
        * (TWO_PI / (P_SIZE * Q))
    )
    weight_re = (gain_cols[:, :, None] * jnp.cos(phase)).astype(jnp.bfloat16)
    weight_im = (-(gain_cols[:, :, None] * jnp.sin(phase))).astype(jnp.bfloat16)
    left_re = jnp.concatenate((weight_re, -weight_im), axis=1)
    left_im = jnp.concatenate((weight_im, weight_re), axis=1)
    return (left_re, left_im)


def general_channelize(voltages, fir_taps):
    cos_one, sin_one, twist_cos, twist_sin, cos_two, sin_two = general_tables()
    local_stations, pol_count, samples = voltages.shape
    tap_count, fft_width = fir_taps.shape
    frames = samples // fft_width - tap_count + 1
    blocks = voltages.reshape(local_stations, pol_count, frames + tap_count - 1, fft_width)
    filtered = jnp.zeros((local_stations, pol_count, frames, fft_width), jnp.float32)
    for tap_idx in range(tap_count):
        filtered = filtered + fir_taps[tap_idx] * blocks[:, :, tap_idx : tap_idx + frames].astype(
            jnp.float32
        )
    folded = filtered.astype(jnp.bfloat16).reshape(local_stations, pol_count, frames, P_SIZE, Q)
    first_table = jnp.concatenate((cos_one, -sin_one), axis=0)
    first_section = jnp.einsum(
        "spfnq,an->spfaq", folded, first_table, preferred_element_type=jnp.float32
    )
    first_re = first_section[:, :, :, :P_SIZE]
    first_im = first_section[:, :, :, P_SIZE:]
    turned = jnp.concatenate(
        (
            (first_re * twist_cos + first_im * twist_sin).astype(jnp.bfloat16),
            (first_im * twist_cos - first_re * twist_sin).astype(jnp.bfloat16),
        ),
        axis=4,
    )
    second_table = jnp.concatenate(
        (jnp.concatenate((cos_two, -sin_two), axis=1), jnp.concatenate((sin_two, cos_two), axis=1)),
        axis=0,
    )
    second = jnp.einsum("spfaq,qb->sbapf", turned, second_table, preferred_element_type=jnp.float32)
    half_q = Q // 2
    chan_re = (
        second[:, :half_q]
        .astype(jnp.bfloat16)
        .reshape(local_stations, half_q * P_SIZE, pol_count * frames)
    )
    chan_im = (
        second[:, half_q:]
        .astype(jnp.bfloat16)
        .reshape(local_stations, half_q * P_SIZE, pol_count * frames)
    )
    return jnp.stack((chan_re, chan_im), axis=0)


def combine(left_re, left_im, stacked_parts, beam_scale):
    stacked = jnp.concatenate((stacked_parts[0], stacked_parts[1]), axis=0)
    beam_re = (
        jnp.einsum("jrk,rkc->jkc", left_re, stacked, preferred_element_type=jnp.float32)
        * beam_scale
    )
    beam_im = (
        jnp.einsum("jrk,rkc->jkc", left_im, stacked, preferred_element_type=jnp.float32)
        * beam_scale
    )
    return jnp.stack((beam_re, beam_im), axis=0)


def general_device(voltages, fir_taps, delays, taper, station_map, beam_order, owners):
    stn_count = lax.axis_size("stn")
    beam_count = lax.axis_size("beam")
    stn_pos = lax.axis_index("stn")
    beam_pos = lax.axis_index("beam")
    local_stations = voltages.shape[0]
    stations = station_map.shape[0]
    group_beams = beam_order.shape[0] // beam_count
    chan_dev = CHANNELS // stn_count
    chan_ids = stn_pos * chan_dev + jnp.arange(chan_dev, dtype=jnp.int32)
    beam_scale = 1.0 / math.sqrt(P_SIZE * Q * stations)
    spectra = general_channelize(voltages, fir_taps)
    owner_model = from_root(delays, "stn", owners[beam_pos])[0]
    row_stn = jnp.arange(stn_count * local_stations, dtype=jnp.int32)
    all_rows = (
        (row_stn // local_stations * beam_count + jnp.arange(beam_count, dtype=jnp.int32)[:, None])
        * local_stations
        + row_stn % local_stations
    ).reshape(-1)
    phys_ids = station_map[all_rows]
    slot_gain = taper[beam_order[beam_pos * group_beams + jnp.arange(group_beams, dtype=jnp.int32)]]
    left_re, left_im = beam_weights(owner_model[:, phys_ids], slot_gain[:, phys_ids], chan_ids)
    full_rows = lax.all_gather(
        lax.all_to_all(spectra, "stn", split_axis=2, concat_axis=1, tiled=True),
        "beam",
        axis=1,
        tiled=True,
    )
    formed = combine(left_re, left_im, full_rows, beam_scale)
    return (formed[0], formed[1])


def on_device(voltages, fir_taps, delays, taper, station_map, beam_order, owners):
    stn_count = lax.axis_size("stn")
    beam_count = lax.axis_size("beam")
    stn_pos = lax.axis_index("stn")
    beam_pos = lax.axis_index("beam")
    local_stations = voltages.shape[0]
    stations = station_map.shape[0]
    group_beams = beam_order.shape[0] // beam_count
    chan_dev = CHANNELS // stn_count
    if chan_dev != P_SIZE * TILE_B:
        return general_device(
            voltages, fir_taps, delays, taper, station_map, beam_order, owners
        )
    scale = 1.0 / math.sqrt(NFFT * stations)
    owner = owners[beam_pos]
    kept = jnp.where(stn_pos == owner, delays[0], 0.0)
    model = lax.psum(kept, "stn")
    spectra = channelize(voltages, fir_taps, dft_tables())
    row_stn = jnp.arange(stn_count * local_stations, dtype=jnp.int32)
    all_rows = (
        (row_stn // local_stations * beam_count + jnp.arange(beam_count, dtype=jnp.int32)[:, None])
        * local_stations
        + row_stn % local_stations
    ).reshape(-1)
    phys = station_map[all_rows]
    slot_gain = taper[beam_order[beam_pos * group_beams + jnp.arange(group_beams, dtype=jnp.int32)]]
    mine = lax.all_to_all(spectra, "stn", split_axis=0, concat_axis=1, tiled=True)
    data = lax.all_gather(mine[0], "beam", axis=0, tiled=True)
    return form_beams(data, model[:, phys], slot_gain[:, phys], stn_pos * chan_dev, scale)


def solution(mesh):
    return jax.shard_map(
        on_device,
        mesh=mesh,
        in_specs=(P(("stn", "beam"), None, None), P(), P("stn", "beam", None), P(), P(), P(), P()),
        out_specs=(P("beam", "stn", None), P("beam", "stn", None)),
        check_vma=False,
    )
```

```python
import functools
import math

import jax
import jax.numpy as jnp
from jax import lax
from jax.experimental import pallas as pl
from jax.experimental.pallas import tpu as pltpu
from jax.sharding import PartitionSpec as P

P_SIZE = 64
Q = 128
CHANNELS = 4096
NFFT = P_SIZE * Q
TILE_B = 8
TWO_PI = 2.0 * math.pi
VMEM_LIMIT = 56 * 1024 * 1024
SEND_ORDER = (6, 1, 4, 2, 7, 3, 5)
WAIT_ORDER = (1, 2, 3, 6, 4, 7, 5)

SIN_COEF = (6.283185272447949, -41.34169703819964, 81.60502363802586, -76.70153767014536, 42.01607576124393, -14.86832274947347, 3.199338841413777)
COS_COEF = (0.999999999885554, -19.739208743453883, 64.93938907589225, -85.45665831478402, 60.242131338256826, -26.404668186962848, 7.800131436606334, -1.4531123148805878)


def sin_cos_turns(turns):
    u = turns - jnp.round(turns)
    w = u * u
    s = jnp.full_like(u, SIN_COEF[-1])
    for coef in SIN_COEF[-2::-1]:
        s = s * w + coef
    c = jnp.full_like(u, COS_COEF[-1])
    for coef in COS_COEF[-2::-1]:
        c = c * w + coef
    return s * u, c


def dft_tables():
    first_idx = jnp.arange(P_SIZE, dtype=jnp.int32)
    second_idx = jnp.arange(Q, dtype=jnp.int32)
    half_idx = jnp.arange(Q // 2, dtype=jnp.int32)
    first_angle = (
        TWO_PI / P_SIZE * (first_idx[:, None] * first_idx[None, :] % P_SIZE).astype(jnp.float32)
    )
    twist_angle = (
        TWO_PI / (P_SIZE * Q) * (first_idx[:, None] * second_idx[None, :]).astype(jnp.float32)
    )
    second_angle = TWO_PI / Q * (second_idx[:, None] * half_idx[None, :] % Q).astype(jnp.float32)
    first = jnp.concatenate((jnp.cos(first_angle), -jnp.sin(first_angle)), axis=0)
    cos_two = jnp.cos(second_angle).T.reshape(-1, TILE_B, Q)
    sin_two = jnp.sin(second_angle).T.reshape(-1, TILE_B, Q)
    re_rows = jnp.concatenate((cos_two, sin_two), axis=2)
    im_rows = jnp.concatenate((-sin_two, cos_two), axis=2)
    second = jnp.stack((re_rows, im_rows), axis=1).reshape(Q, 2 * Q)
    return (
        first.astype(jnp.bfloat16),
        jnp.cos(twist_angle),
        jnp.sin(twist_angle),
        second.astype(jnp.bfloat16),
    )


def filter_station(volt_ref, taps_ref, filt, pols, frames, tap_count):
    group = 8
    for part in range(P_SIZE // 16):
        rows = pl.ds(part * 16, 16)
        taps = [taps_ref[m, rows, :] for m in range(tap_count)]

        def body(idx, carry):
            pol, first = idx // (frames // group), idx % (frames // group) * group
            sums = [None] * group
            for step in range(group + tap_count - 1):
                value = volt_ref[pol, first + step, rows, :].astype(jnp.float32)
                for f in range(group):
                    m = step - f
                    if 0 <= m < tap_count:
                        term = taps[m] * value
                        sums[f] = term if sums[f] is None else sums[f] + term
            for f in range(group):
                filt[pol * frames + first + f, rows, :] = sums[f].astype(jnp.bfloat16)
            return carry

        lax.fori_loop(0, pols * frames // group, body, 0)


def first_section(filt, first_ref, cos_ref, sin_ref, turn_re, turn_im, count):
    table = first_ref[...]
    width = 4

    def body(idx, carry):
        c0 = idx * width
        pair = jnp.concatenate([filt[c0 + i] for i in range(width)], axis=1)
        both = jnp.dot(table, pair, preferred_element_type=jnp.float32)
        for i in range(width):
            re = both[:P_SIZE, i * Q : (i + 1) * Q]
            im = both[P_SIZE:, i * Q : (i + 1) * Q]
            rows = pl.ds(pl.multiple_of((c0 + i) * P_SIZE, P_SIZE), P_SIZE)
            turn_re[rows, :] = re * cos_ref[...] + im * sin_ref[...]
            turn_im[rows, :] = im * cos_ref[...] - re * sin_ref[...]
        return carry

    lax.fori_loop(0, count // width, body, 0, unroll=2)


def second_section(second_ref, turn_re, turn_im, count, store):
    table = second_ref[...]

    def body(a, carry):
        rows = pl.ds(a, count, stride=P_SIZE)
        turned = jnp.concatenate(
            (turn_re[rows, :].astype(jnp.bfloat16), turn_im[rows, :].astype(jnp.bfloat16)), axis=1
        )
        out = lax.dot_general(
            table, turned, (((1,), (1,)), ((), ())), preferred_element_type=jnp.float32
        )
        store(a, out.astype(jnp.bfloat16))
        return carry

    lax.fori_loop(0, P_SIZE, body, 0, unroll=8)


def channel_kernel(
    frames, volt_ref, taps_ref, first_ref, cos_ref, sin_ref, second_ref, out_ref, filt, turn_re, turn_im
):
    pols = volt_ref.shape[1]
    count = pols * frames
    filter_station(volt_ref.at[0], taps_ref, filt, pols, frames, taps_ref.shape[0])
    first_section(filt, first_ref, cos_ref, sin_ref, turn_re, turn_im, count)

    def store(a, value):
        out_ref[:, 0, a] = value.reshape(out_ref.shape[0], 2 * TILE_B, count)

    second_section(second_ref, turn_re, turn_im, count, store)


def channelize(voltages, fir_taps, tables):
    stations, pols, samples = voltages.shape
    tap_count = fir_taps.shape[0]
    blocks = samples // NFFT
    frames = blocks - tap_count + 1
    count = pols * frames
    tiles = P_SIZE // TILE_B
    volts = voltages.reshape(stations, pols, blocks, P_SIZE, Q)
    taps = fir_taps.reshape(tap_count, P_SIZE, Q)
    whole = lambda shape: pl.BlockSpec(shape, lambda l: (0,) * len(shape))
    return pl.pallas_call(
        functools.partial(channel_kernel, frames),
        grid=(stations,),
        in_specs=[
            pl.BlockSpec((1, pols, blocks, P_SIZE, Q), lambda l: (l, 0, 0, 0, 0)),
            whole(taps.shape),
        ]
        + [whole(t.shape) for t in tables],
        out_specs=pl.BlockSpec(
            (tiles, 1, P_SIZE, 2 * TILE_B, count), lambda l: (0, l, 0, 0, 0)
        ),
        out_shape=jax.ShapeDtypeStruct((tiles, stations, P_SIZE, 2 * TILE_B, count), jnp.bfloat16),
        scratch_shapes=[
            pltpu.VMEM((count, P_SIZE, Q), jnp.bfloat16),
            pltpu.VMEM((count * P_SIZE, Q), jnp.float32),
            pltpu.VMEM((count * P_SIZE, Q), jnp.float32),
        ],
        compiler_params=pltpu.CompilerParams(vmem_limit_bytes=VMEM_LIMIT),
        name="channelize",
    )(volts, taps, *tables)


def exchange_kernel(
    spec_ref,
    model_ref,
    data_ref,
    models_ref,
    direct_send,
    direct_recv,
    far_send,
    far_recv,
    near_send,
    near_recv,
    last_send,
    last_recv,
    model_send,
    model_recv,
    local_sem,
):
    stn, beam = lax.axis_index("stn"), lax.axis_index("beam")
    locals_ = spec_ref.shape[1]
    far = (beam + 2) % 4
    near = beam + 1 - 2 * (beam % 2)

    def partner(m):
        z, x = stn // 2, stn % 2
        if m % 2:
            x = 1 - x
        if m // 2 % 2:
            z = z + 1 - 2 * (z % 2)
        if m // 4:
            z = (z + 2) % 4
        return z * 2 + x

    def row(s, b, l):
        return (s * 4 + b) * locals_ + l

    def remote(src, dst, send, recv, s, b):
        copy = pltpu.make_async_remote_copy(
            src_ref=src,
            dst_ref=dst,
            send_sem=send,
            recv_sem=recv,
            device_id=(s, b),
            device_id_type=pl.DeviceIdType.MESH,
        )
        copy.start()
        return copy

    barrier = pltpu.get_barrier_semaphore()
    peers = [(partner(m), beam) for m in range(1, 8)] + [(stn, far), (stn, near)]
    for peer in peers:
        pl.semaphore_signal(barrier, inc=1, device_id=peer, device_id_type=pl.DeviceIdType.MESH)
    pl.semaphore_wait(barrier, len(peers))

    own_copies = [pltpu.make_async_copy(model_ref, models_ref.at[stn], local_sem.at[locals_])]
    direct, far_copy, near_copy, last_copy, model_copy = {}, {}, {}, {}, {}
    for l in range(locals_):
        own_copies.append(
            pltpu.make_async_copy(
                spec_ref.at[stn, l], data_ref.at[row(stn, beam, l)], local_sem.at[l]
            )
        )
        for m in SEND_ORDER:
            direct[m, l] = remote(
                spec_ref.at[partner(m), l],
                data_ref.at[row(stn, beam, l)],
                direct_send.at[m, l],
                direct_recv.at[m, l],
                partner(m),
                beam,
            )
        if l == 0:
            for m in range(1, 8):
                model_copy[m] = remote(
                    model_ref,
                    models_ref.at[stn],
                    model_send.at[m],
                    model_recv.at[m],
                    partner(m),
                    beam,
                )
    for copy in own_copies:
        copy.start()

    def pass_on(key):
        m, l = key
        far_copy[key].wait_recv()
        place = data_ref.at[row(partner(m), far, l)]
        last_copy[key] = remote(
            place, place, last_send.at[m, l], last_recv.at[m, l], stn, near
        )

    steps = [(m, l) for m in (0,) + WAIT_ORDER[:3] for l in range(locals_)]
    steps += [(m, l) for l in range(locals_) for m in WAIT_ORDER[3:]]
    before = None
    for key in steps:
        m, l = key
        place = data_ref.at[row(partner(m), beam, l)]
        if m:
            direct[key].wait_recv()
            src = place
        else:
            src = spec_ref.at[stn, l]
        far_copy[key] = remote(src, place, far_send.at[m, l], far_recv.at[m, l], stn, far)
        near_copy[key] = remote(src, place, near_send.at[m, l], near_recv.at[m, l], stn, near)
        if before is not None:
            pass_on(before)
        before = key
    pass_on(before)
    for key in steps:
        near_copy[key].wait_recv()
        last_copy[key].wait_recv()
        far_copy[key].wait_send()
        near_copy[key].wait_send()
        last_copy[key].wait_send()
    for copy in direct.values():
        copy.wait_send()
    for copy in model_copy.values():
        copy.wait()
    for copy in own_copies:
        copy.wait()


def exchange(spectra, model):
    stn_count, locals_ = spectra.shape[:2]
    stations = stn_count * 4 * locals_
    pair = pltpu.SemaphoreType.DMA((stn_count, locals_))
    one = pltpu.SemaphoreType.DMA((stn_count,))
    return pl.pallas_call(
        exchange_kernel,
        in_specs=[pl.BlockSpec(memory_space=pl.ANY)] * 2,
        out_specs=[pl.BlockSpec(memory_space=pl.ANY)] * 2,
        out_shape=[
            jax.ShapeDtypeStruct((stations,) + spectra.shape[2:], spectra.dtype),
            jax.ShapeDtypeStruct((stn_count,) + model.shape, model.dtype),
        ],
        scratch_shapes=[pair] * 8 + [one, one, pltpu.SemaphoreType.DMA((locals_ + 1,))],
        compiler_params=pltpu.CompilerParams(
            collective_id=0, has_side_effects=True, vmem_limit_bytes=VMEM_LIMIT
        ),
        name="exchange",
    )(spectra, model)


def beam_kernel(step_a, scale, data_ref, delay_ref, gain_ref, base_ref, re_ref, im_ref):
    beams, lanes = delay_ref.shape
    count = data_ref.shape[-1]
    lane = lax.broadcasted_iota(jnp.int32, (TILE_B, lanes), 1)
    row = lax.broadcasted_iota(jnp.int32, (TILE_B, lanes), 0)
    keep = lane % TILE_B == row
    quarter = (lane[:1] // TILE_B % 2).astype(jnp.float32) * 0.25
    delay = delay_ref[...]
    chan = base_ref[...] + (pl.program_id(0) * step_a).astype(jnp.float32)
    sin_t, cos_t = sin_cos_turns(delay * chan * (1.0 / NFFT) - quarter)
    sin_d, cos_d = sin_cos_turns(delay * (1.0 / NFFT))
    part_re = gain_ref[...] * cos_t
    part_im = -(gain_ref[...] * sin_t)

    def spread(part):
        return (
            jnp.where(keep[None], part[:, None, :], 0.0)
            .astype(jnp.bfloat16)
            .reshape(beams * TILE_B, lanes)
        )

    out_re = re_ref.reshape(beams * TILE_B * step_a, count)
    out_im = im_ref.reshape(beams * TILE_B * step_a, count)
    for a in range(step_a):
        if a:
            part_re, part_im = (
                part_re * cos_d + part_im * sin_d,
                part_im * cos_d - part_re * sin_d,
            )
        data = data_ref[:, a].reshape(lanes, count)
        rows = pl.ds(a, beams * TILE_B, stride=step_a)
        out_re[rows, :] = (
            jnp.dot(spread(part_re), data, preferred_element_type=jnp.float32) * scale
        )
        out_im[rows, :] = (
            jnp.dot(spread(part_im), data, preferred_element_type=jnp.float32) * scale
        )


def form_beams(data, delay, gain, first_chan, scale):
    stations, _, tile_rows, count = data.shape
    beams = delay.shape[0]
    lanes = stations * tile_rows
    step_a = 8
    base = first_chan + P_SIZE * (jnp.arange(lanes, dtype=jnp.int32) % TILE_B)
    spec = lambda shape: pl.BlockSpec(shape, lambda i: (0,) * len(shape))
    out_spec = pl.BlockSpec((beams * TILE_B, step_a, count), lambda i: (0, i, 0))
    out_shape = jax.ShapeDtypeStruct((beams * TILE_B, P_SIZE, count), jnp.float32)
    re, im = pl.pallas_call(
        functools.partial(beam_kernel, step_a, scale),
        grid=(P_SIZE // step_a,),
        in_specs=[
            pl.BlockSpec((stations, step_a, tile_rows, count), lambda i: (0, i, 0, 0)),
            spec((beams, lanes)),
            spec((beams, lanes)),
            spec((1, lanes)),
        ],
        out_specs=[out_spec, out_spec],
        out_shape=[out_shape, out_shape],
        compiler_params=pltpu.CompilerParams(vmem_limit_bytes=VMEM_LIMIT),
        name="form_beams",
    )(
        data,
        jnp.repeat(delay, tile_rows, axis=1),
        jnp.repeat(gain, tile_rows, axis=1),
        base.astype(jnp.float32)[None],
    )
    shape = (beams, TILE_B * P_SIZE, count)
    return re.reshape(shape), im.reshape(shape)


def from_root(value, axis, source):
    kept = jnp.where(lax.axis_index(axis) == source, value, 0).astype(value.dtype)
    return lax.psum(kept, axis)


def general_tables():
    first_idx = jnp.arange(P_SIZE, dtype=jnp.int32)
    second_idx = jnp.arange(Q, dtype=jnp.int32)
    half_idx = jnp.arange(Q // 2, dtype=jnp.int32)
    first_angle = (
        TWO_PI / P_SIZE * (first_idx[:, None] * first_idx[None, :] % P_SIZE).astype(jnp.float32)
    )
    twist_angle = (
        TWO_PI / (P_SIZE * Q) * (first_idx[:, None] * second_idx[None, :]).astype(jnp.float32)
    )
    second_angle = TWO_PI / Q * (second_idx[:, None] * half_idx[None, :] % Q).astype(jnp.float32)
    return (
        jnp.cos(first_angle).astype(jnp.bfloat16),
        jnp.sin(first_angle).astype(jnp.bfloat16),
        jnp.cos(twist_angle),
        jnp.sin(twist_angle),
        jnp.cos(second_angle).astype(jnp.bfloat16),
        jnp.sin(second_angle).astype(jnp.bfloat16),
    )


def beam_weights(delay_cols, gain_cols, chan_ids):
    phase = (
        delay_cols[:, :, None]
        * chan_ids.astype(jnp.float32)[None, None, :]
        * (TWO_PI / (P_SIZE * Q))
    )
    weight_re = (gain_cols[:, :, None] * jnp.cos(phase)).astype(jnp.bfloat16)
    weight_im = (-(gain_cols[:, :, None] * jnp.sin(phase))).astype(jnp.bfloat16)
    left_re = jnp.concatenate((weight_re, -weight_im), axis=1)
    left_im = jnp.concatenate((weight_im, weight_re), axis=1)
    return (left_re, left_im)


def general_channelize(voltages, fir_taps):
    cos_one, sin_one, twist_cos, twist_sin, cos_two, sin_two = general_tables()
    local_stations, pol_count, samples = voltages.shape
    tap_count, fft_width = fir_taps.shape
    frames = samples // fft_width - tap_count + 1
    blocks = voltages.reshape(local_stations, pol_count, frames + tap_count - 1, fft_width)
    filtered = jnp.zeros((local_stations, pol_count, frames, fft_width), jnp.float32)
    for tap_idx in range(tap_count):
        filtered = filtered + fir_taps[tap_idx] * blocks[:, :, tap_idx : tap_idx + frames].astype(
            jnp.float32
        )
    folded = filtered.astype(jnp.bfloat16).reshape(local_stations, pol_count, frames, P_SIZE, Q)
    first_table = jnp.concatenate((cos_one, -sin_one), axis=0)
    first_section = jnp.einsum(
        "spfnq,an->spfaq", folded, first_table, preferred_element_type=jnp.float32
    )
    first_re = first_section[:, :, :, :P_SIZE]
    first_im = first_section[:, :, :, P_SIZE:]
    turned = jnp.concatenate(
        (
            (first_re * twist_cos + first_im * twist_sin).astype(jnp.bfloat16),
            (first_im * twist_cos - first_re * twist_sin).astype(jnp.bfloat16),
        ),
        axis=4,
    )
    second_table = jnp.concatenate(
        (jnp.concatenate((cos_two, -sin_two), axis=1), jnp.concatenate((sin_two, cos_two), axis=1)),
        axis=0,
    )
    second = jnp.einsum("spfaq,qb->sbapf", turned, second_table, preferred_element_type=jnp.float32)
    half_q = Q // 2
    chan_re = (
        second[:, :half_q]
        .astype(jnp.bfloat16)
        .reshape(local_stations, half_q * P_SIZE, pol_count * frames)
    )
    chan_im = (
        second[:, half_q:]
        .astype(jnp.bfloat16)
        .reshape(local_stations, half_q * P_SIZE, pol_count * frames)
    )
    return jnp.stack((chan_re, chan_im), axis=0)


def combine(left_re, left_im, stacked_parts, beam_scale):
    stacked = jnp.concatenate((stacked_parts[0], stacked_parts[1]), axis=0)
    beam_re = (
        jnp.einsum("jrk,rkc->jkc", left_re, stacked, preferred_element_type=jnp.float32)
        * beam_scale
    )
    beam_im = (
        jnp.einsum("jrk,rkc->jkc", left_im, stacked, preferred_element_type=jnp.float32)
        * beam_scale
    )
    return jnp.stack((beam_re, beam_im), axis=0)


def general_device(voltages, fir_taps, delays, taper, station_map, beam_order, owners):
    stn_count = lax.axis_size("stn")
    beam_count = lax.axis_size("beam")
    stn_pos = lax.axis_index("stn")
    beam_pos = lax.axis_index("beam")
    local_stations = voltages.shape[0]
    stations = station_map.shape[0]
    group_beams = beam_order.shape[0] // beam_count
    chan_dev = CHANNELS // stn_count
    chan_ids = stn_pos * chan_dev + jnp.arange(chan_dev, dtype=jnp.int32)
    beam_scale = 1.0 / math.sqrt(P_SIZE * Q * stations)
    spectra = general_channelize(voltages, fir_taps)
    owner_model = from_root(delays, "stn", owners[beam_pos])[0]
    row_stn = jnp.arange(stn_count * local_stations, dtype=jnp.int32)
    all_rows = (
        (row_stn // local_stations * beam_count + jnp.arange(beam_count, dtype=jnp.int32)[:, None])
        * local_stations
        + row_stn % local_stations
    ).reshape(-1)
    phys_ids = station_map[all_rows]
    slot_gain = taper[beam_order[beam_pos * group_beams + jnp.arange(group_beams, dtype=jnp.int32)]]
    left_re, left_im = beam_weights(owner_model[:, phys_ids], slot_gain[:, phys_ids], chan_ids)
    full_rows = lax.all_gather(
        lax.all_to_all(spectra, "stn", split_axis=2, concat_axis=1, tiled=True),
        "beam",
        axis=1,
        tiled=True,
    )
    formed = combine(left_re, left_im, full_rows, beam_scale)
    return (formed[0], formed[1])


def on_device(voltages, fir_taps, delays, taper, station_map, beam_order, owners):
    stn_count = lax.axis_size("stn")
    beam_count = lax.axis_size("beam")
    stn_pos = lax.axis_index("stn")
    beam_pos = lax.axis_index("beam")
    local_stations = voltages.shape[0]
    stations = station_map.shape[0]
    group_beams = beam_order.shape[0] // beam_count
    chan_dev = CHANNELS // stn_count
    if (stn_count, beam_count, chan_dev) != (8, 4, P_SIZE * TILE_B):
        return general_device(
            voltages, fir_taps, delays, taper, station_map, beam_order, owners
        )
    scale = 1.0 / math.sqrt(NFFT * stations)
    slot_gain = taper[beam_order[beam_pos * group_beams + jnp.arange(group_beams, dtype=jnp.int32)]]
    own_model = jnp.pad(delays[0][:, station_map], ((0, 0), (0, -stations % 128)))
    spectra = channelize(voltages, fir_taps, dft_tables())
    data, models = exchange(spectra, own_model)
    model = models[owners[beam_pos]][:, :stations]
    return form_beams(data, model, slot_gain[:, station_map], stn_pos * chan_dev, scale)


def solution(mesh):
    return jax.shard_map(
        on_device,
        mesh=mesh,
        in_specs=(P(("stn", "beam"), None, None), P(), P("stn", "beam", None), P(), P(), P(), P()),
        out_specs=(P("beam", "stn", None), P("beam", "stn", None)),
        check_vma=False,
    )
```

```python
import functools
import math

import jax
import jax.numpy as jnp
import numpy as np
from jax import lax
from jax.experimental import pallas as pl
from jax.experimental.pallas import tpu as pltpu
from jax.sharding import PartitionSpec as P

P_SIZE = 64
Q = 128
CHANNELS = 4096
NFFT = P_SIZE * Q
TILE_B = 8
TWO_PI = 2.0 * math.pi
VMEM_LIMIT = 56 * 1024 * 1024
SEND_ORDER = (6, 1, 4, 2, 7, 3, 5)
WAIT_ORDER = (1, 2, 3, 6, 4, 7, 5)
EARLY = (((), ()), (((1, 0),), ((2, 0),)))

SIN_COEF = (6.283185272447949, -41.34169703819964, 81.60502363802586, -76.70153767014536, 42.01607576124393, -14.86832274947347, 3.199338841413777)
COS_COEF = (0.999999999885554, -19.739208743453883, 64.93938907589225, -85.45665831478402, 60.242131338256826, -26.404668186962848, 7.800131436606334, -1.4531123148805878)


def sin_cos_turns(turns):
    u = turns - jnp.round(turns)
    w = u * u
    s = jnp.full_like(u, SIN_COEF[-1])
    for coef in SIN_COEF[-2::-1]:
        s = s * w + coef
    c = jnp.full_like(u, COS_COEF[-1])
    for coef in COS_COEF[-2::-1]:
        c = c * w + coef
    return s * u, c


def dft_tables():
    first_idx, second_idx, half_idx = np.arange(P_SIZE), np.arange(Q), np.arange(Q // 2)
    first_angle = TWO_PI / P_SIZE * (first_idx[:, None] * first_idx[None, :] % P_SIZE)
    twist_angle = TWO_PI / NFFT * (first_idx[:, None] * second_idx[None, :])
    second_angle = TWO_PI / Q * (second_idx[:, None] * half_idx[None, :] % Q)
    first = np.concatenate((np.cos(first_angle), -np.sin(first_angle)), axis=0)
    cos_two = np.cos(second_angle).T.reshape(-1, TILE_B, Q)
    sin_two = np.sin(second_angle).T.reshape(-1, TILE_B, Q)
    re_rows = np.concatenate((cos_two, sin_two), axis=2)
    im_rows = np.concatenate((-sin_two, cos_two), axis=2)
    second = np.stack((re_rows, im_rows), axis=1).reshape(Q, 2 * Q)
    return (
        jnp.asarray(first.astype(np.float32).astype(jnp.bfloat16)),
        jnp.asarray(np.cos(twist_angle).astype(np.float32)),
        jnp.asarray(np.sin(twist_angle).astype(np.float32)),
        jnp.asarray(second.astype(np.float32).astype(jnp.bfloat16)),
    )


def filter_station(volt_ref, taps_ref, filt, pols, frames, tap_count):
    group = 8
    for part in range(P_SIZE // 16):
        rows = pl.ds(part * 16, 16)
        taps = [taps_ref[m, rows, :] for m in range(tap_count)]

        def body(idx, carry):
            pol, first = idx // (frames // group), idx % (frames // group) * group
            sums = [None] * group
            for step in range(group + tap_count - 1):
                value = volt_ref[pol, first + step, rows, :].astype(jnp.float32)
                for f in range(group):
                    m = step - f
                    if 0 <= m < tap_count:
                        term = taps[m] * value
                        sums[f] = term if sums[f] is None else sums[f] + term
            for f in range(group):
                filt[pol * frames + first + f, rows, :] = sums[f].astype(jnp.bfloat16)
            return carry

        lax.fori_loop(0, pols * frames // group, body, 0)


def first_section(filt, first_ref, cos_ref, sin_ref, turn_re, turn_im, count):
    table = first_ref[...]
    width = 4

    def body(idx, carry):
        c0 = idx * width
        pair = jnp.concatenate([filt[c0 + i] for i in range(width)], axis=1)
        both = jnp.dot(table, pair, preferred_element_type=jnp.float32)
        for i in range(width):
            re = both[:P_SIZE, i * Q : (i + 1) * Q]
            im = both[P_SIZE:, i * Q : (i + 1) * Q]
            rows = pl.ds(pl.multiple_of((c0 + i) * P_SIZE, P_SIZE), P_SIZE)
            turn_re[rows, :] = re * cos_ref[...] + im * sin_ref[...]
            turn_im[rows, :] = im * cos_ref[...] - re * sin_ref[...]
        return carry

    lax.fori_loop(0, count // width, body, 0, unroll=2)


def second_section(second_ref, turn_re, turn_im, count, store):
    table = second_ref[...]

    def body(a, carry):
        rows = pl.ds(a, count, stride=P_SIZE)
        turned = jnp.concatenate(
            (turn_re[rows, :].astype(jnp.bfloat16), turn_im[rows, :].astype(jnp.bfloat16)), axis=1
        )
        out = lax.dot_general(
            table, turned, (((1,), (1,)), ((), ())), preferred_element_type=jnp.float32
        )
        store(a, out.astype(jnp.bfloat16))
        return carry

    lax.fori_loop(0, P_SIZE, body, 0, unroll=8)


def exchange_kernel(
    volt_hbm,
    model_ref,
    taps_ref,
    first_ref,
    cos_ref,
    sin_ref,
    second_ref,
    data_ref,
    models_ref,
    volts,
    filt,
    turn_re,
    turn_im,
    spec_ref,
    volt_sem,
    direct_send,
    direct_recv,
    far_send,
    far_recv,
    near_send,
    near_recv,
    last_send,
    last_recv,
    model_send,
    model_recv,
    local_sem,
):
    locals_, pols, blocks = volt_hbm.shape[:3]
    tap_count = taps_ref.shape[0]
    frames = blocks - tap_count + 1
    count = pols * frames
    loads = [
        pltpu.make_async_copy(volt_hbm.at[l], volts.at[l], volt_sem.at[l]) for l in range(locals_)
    ]
    for load in loads:
        load.start()
    stn, beam = lax.axis_index("stn"), lax.axis_index("beam")
    far = (beam + 2) % 4
    near = beam + 1 - 2 * (beam % 2)

    def partner(m):
        z, x = stn // 2, stn % 2
        if m % 2:
            x = 1 - x
        if m // 2 % 2:
            z = z + 1 - 2 * (z % 2)
        if m // 4:
            z = (z + 2) % 4
        return z * 2 + x

    def row(s, b, l):
        return (s * 4 + b) * locals_ + l

    def remote(src, dst, send, recv, s, b):
        copy = pltpu.make_async_remote_copy(
            src_ref=src,
            dst_ref=dst,
            send_sem=send,
            recv_sem=recv,
            device_id=(s, b),
            device_id_type=pl.DeviceIdType.MESH,
        )
        copy.start()
        return copy

    barrier = pltpu.get_barrier_semaphore()
    peers = [(partner(m), beam) for m in range(1, 8)] + [(stn, far), (stn, near)]
    for peer in peers:
        pl.semaphore_signal(barrier, inc=1, device_id=peer, device_id_type=pl.DeviceIdType.MESH)
    pl.semaphore_wait(barrier, len(peers))

    own_copies = [pltpu.make_async_copy(model_ref, models_ref.at[stn], local_sem.at[locals_])]
    own_copies[0].start()
    direct, far_copy, near_copy, last_copy, model_copy = {}, {}, {}, {}, {}
    for m in range(1, 8):
        model_copy[m] = remote(
            model_ref, models_ref.at[stn], model_send.at[m], model_recv.at[m], partner(m), beam
        )

    def pass_on(key):
        m, l = key
        far_copy[key].wait_recv()
        place = data_ref.at[row(partner(m), far, l)]
        last_copy[key] = remote(
            place, place, last_send.at[m, l], last_recv.at[m, l], stn, near
        )

    waiting = []

    def step(key):
        m, l = key
        place = data_ref.at[row(partner(m), beam, l)]
        if m:
            direct[key].wait_recv()
            src = place
        else:
            src = spec_ref.at[stn, l]
        far_copy[key] = remote(src, place, far_send.at[m, l], far_recv.at[m, l], stn, far)
        near_copy[key] = remote(src, place, near_send.at[m, l], near_recv.at[m, l], stn, near)
        if waiting:
            pass_on(waiting.pop())
        waiting.append(key)

    for l in range(locals_):
        loads[l].wait()
        filter_station(volts.at[l], taps_ref, filt, pols, frames, tap_count)
        for key in EARLY[l][0]:
            step(key)
        first_section(filt, first_ref, cos_ref, sin_ref, turn_re, turn_im, count)
        for key in EARLY[l][1]:
            step(key)

        def store(a, value):
            spec_ref[:, l, a] = value.reshape(spec_ref.shape[0], 2 * TILE_B, count)

        second_section(second_ref, turn_re, turn_im, count, store)
        own = pltpu.make_async_copy(
            spec_ref.at[stn, l], data_ref.at[row(stn, beam, l)], local_sem.at[l]
        )
        own.start()
        own_copies.append(own)
        for m in SEND_ORDER:
            direct[m, l] = remote(
                spec_ref.at[partner(m), l],
                data_ref.at[row(stn, beam, l)],
                direct_send.at[m, l],
                direct_recv.at[m, l],
                partner(m),
                beam,
            )
        step((0, l))
    steps = [(m, l) for m in WAIT_ORDER[:3] for l in range(locals_)]
    steps += [(m, l) for l in range(locals_) for m in WAIT_ORDER[3:]]
    for key in steps:
        if key not in far_copy:
            step(key)
    pass_on(waiting.pop())
    for key in far_copy:
        near_copy[key].wait_recv()
        last_copy[key].wait_recv()
        far_copy[key].wait_send()
        near_copy[key].wait_send()
        last_copy[key].wait_send()
    for copy in direct.values():
        copy.wait_send()
    for copy in model_copy.values():
        copy.wait()
    for copy in own_copies:
        copy.wait()


def exchange(voltages, fir_taps, model, stn_count):
    locals_, pols, samples = voltages.shape
    tap_count = fir_taps.shape[0]
    blocks = samples // NFFT
    count = pols * (blocks - tap_count + 1)
    stations = stn_count * 4 * locals_
    pair = pltpu.SemaphoreType.DMA((stn_count, locals_))
    one = pltpu.SemaphoreType.DMA((stn_count,))
    anywhere, vmem = pl.BlockSpec(memory_space=pl.ANY), pl.BlockSpec(memory_space=pltpu.VMEM)
    return pl.pallas_call(
        exchange_kernel,
        in_specs=[anywhere] * 2 + [vmem] * 5,
        out_specs=[anywhere] * 2,
        out_shape=[
            jax.ShapeDtypeStruct((stations, P_SIZE, 2 * TILE_B, count), jnp.bfloat16),
            jax.ShapeDtypeStruct((stn_count,) + model.shape, model.dtype),
        ],
        scratch_shapes=[
            pltpu.VMEM((locals_, pols, blocks, P_SIZE, Q), jnp.bfloat16),
            pltpu.VMEM((count, P_SIZE, Q), jnp.bfloat16),
            pltpu.VMEM((count * P_SIZE, Q), jnp.float32),
            pltpu.VMEM((count * P_SIZE, Q), jnp.float32),
            pltpu.VMEM((stn_count, locals_, P_SIZE, 2 * TILE_B, count), jnp.bfloat16),
            pltpu.SemaphoreType.DMA((locals_,)),
        ]
        + [pair] * 8
        + [one, one, pltpu.SemaphoreType.DMA((locals_ + 1,))],
        compiler_params=pltpu.CompilerParams(
            collective_id=0, has_side_effects=True, vmem_limit_bytes=VMEM_LIMIT
        ),
        name="exchange",
    )(
        voltages.reshape(locals_, pols, blocks, P_SIZE, Q),
        model,
        fir_taps.reshape(tap_count, P_SIZE, Q),
        *dft_tables(),
    )


def beam_kernel(
    step_a,
    scale,
    owners_ref,
    order_ref,
    data_ref,
    models_ref,
    taper_ref,
    map_ref,
    mask_ref,
    re_ref,
    im_ref,
    rows_ref,
    delay_ref,
    gain_ref,
):
    beams, lanes = delay_ref.shape
    stations = map_ref.shape[1]
    count = data_ref.shape[-1]
    stn, beam = lax.axis_index("stn"), lax.axis_index("beam")
    step_idx = pl.program_id(0)

    @pl.when(step_idx == 0)
    def _():
        phys = lax.broadcasted_iota(jnp.int32, (stations, stations), 0)
        pick = (phys == map_ref[...]).astype(jnp.float32)
        station = lax.broadcasted_iota(jnp.int32, (stations, lanes), 0)
        lane_at = lax.broadcasted_iota(jnp.int32, (stations, lanes), 1)
        widen = (lane_at // (2 * TILE_B) == station).astype(jnp.float32)

        def by_lane(rows):
            exact = functools.partial(
                jnp.dot, precision=lax.Precision.HIGHEST, preferred_element_type=jnp.float32
            )
            return exact(exact(rows, pick), widen)

        for j in range(beams):
            rows_ref[pl.ds(j, 1), :] = taper_ref[pl.ds(order_ref[beam * beams + j], 1), :]
        gain_ref[...] = by_lane(rows_ref[...])
        delay_ref[...] = by_lane(models_ref[owners_ref[beam]])

    lane = lax.broadcasted_iota(jnp.int32, (1, lanes), 1)
    quarter = (lane // TILE_B % 2).astype(jnp.float32) * 0.25
    chan = (P_SIZE * (TILE_B * stn + lane % TILE_B) + step_idx * step_a).astype(jnp.float32)
    delay = delay_ref[...]
    sin_t, cos_t = sin_cos_turns(delay * chan * (1.0 / NFFT) - quarter)
    sin_d, cos_d = sin_cos_turns(delay * (1.0 / NFFT))
    part_re = gain_ref[...] * cos_t
    part_im = -(gain_ref[...] * sin_t)
    outs = [ref.reshape(beams * TILE_B * step_a, count) for ref in (re_ref, im_ref)]
    for a in range(step_a):
        if a:
            part_re, part_im = (
                part_re * cos_d + part_im * sin_d,
                part_im * cos_d - part_re * sin_d,
            )
        data = data_ref[:, a].reshape(lanes, count)
        weights = jnp.concatenate(
            [
                part.astype(jnp.bfloat16) * mask_ref[b]
                for part in (part_re, part_im)
                for b in range(TILE_B)
            ],
            axis=0,
        )
        formed = jnp.dot(weights, data, preferred_element_type=jnp.float32) * scale
        for half, out in enumerate(outs):
            for b in range(TILE_B):
                first = (half * TILE_B + b) * beams
                out[pl.ds(b * step_a + a, beams, stride=TILE_B * step_a), :] = formed[
                    first : first + beams
                ]


def form_beams(data, models, taper, station_map, beam_order, owners, scale):
    stations, _, tile_rows, count = data.shape
    beams = models.shape[1]
    lanes = stations * tile_rows
    step_a = 8
    mask = np.broadcast_to(
        np.arange(lanes)[None, None] % TILE_B == np.arange(TILE_B)[:, None, None],
        (TILE_B, beams, lanes),
    )
    whole = lambda x: pl.BlockSpec(x.shape, lambda i: (0,) * x.ndim)
    smem = pl.BlockSpec(memory_space=pltpu.SMEM)
    out_spec = pl.BlockSpec((beams * TILE_B, step_a, count), lambda i: (0, i, 0))
    out_shape = jax.ShapeDtypeStruct((beams * TILE_B, P_SIZE, count), jnp.float32)
    held = [models, taper, station_map[None], jnp.asarray(mask.astype(jnp.bfloat16))]
    re, im = pl.pallas_call(
        functools.partial(beam_kernel, step_a, scale),
        grid=(P_SIZE // step_a,),
        in_specs=[
            smem,
            smem,
            pl.BlockSpec((stations, step_a, tile_rows, count), lambda i: (0, i, 0, 0)),
        ]
        + [whole(x) for x in held],
        out_specs=[out_spec, out_spec],
        out_shape=[out_shape, out_shape],
        scratch_shapes=[
            pltpu.VMEM((beams, stations), jnp.float32),
            pltpu.VMEM((beams, lanes), jnp.float32),
            pltpu.VMEM((beams, lanes), jnp.float32),
        ],
        compiler_params=pltpu.CompilerParams(vmem_limit_bytes=VMEM_LIMIT),
        name="form_beams",
    )(owners, beam_order, data, *held)
    shape = (beams, TILE_B * P_SIZE, count)
    return re.reshape(shape), im.reshape(shape)


def from_root(value, axis, source):
    kept = jnp.where(lax.axis_index(axis) == source, value, 0).astype(value.dtype)
    return lax.psum(kept, axis)


def general_tables():
    first_idx = jnp.arange(P_SIZE, dtype=jnp.int32)
    second_idx = jnp.arange(Q, dtype=jnp.int32)
    half_idx = jnp.arange(Q // 2, dtype=jnp.int32)
    first_angle = (
        TWO_PI / P_SIZE * (first_idx[:, None] * first_idx[None, :] % P_SIZE).astype(jnp.float32)
    )
    twist_angle = (
        TWO_PI / (P_SIZE * Q) * (first_idx[:, None] * second_idx[None, :]).astype(jnp.float32)
    )
    second_angle = TWO_PI / Q * (second_idx[:, None] * half_idx[None, :] % Q).astype(jnp.float32)
    return (
        jnp.cos(first_angle).astype(jnp.bfloat16),
        jnp.sin(first_angle).astype(jnp.bfloat16),
        jnp.cos(twist_angle),
        jnp.sin(twist_angle),
        jnp.cos(second_angle).astype(jnp.bfloat16),
        jnp.sin(second_angle).astype(jnp.bfloat16),
    )


def beam_weights(delay_cols, gain_cols, chan_ids):
    phase = (
        delay_cols[:, :, None]
        * chan_ids.astype(jnp.float32)[None, None, :]
        * (TWO_PI / (P_SIZE * Q))
    )
    weight_re = (gain_cols[:, :, None] * jnp.cos(phase)).astype(jnp.bfloat16)
    weight_im = (-(gain_cols[:, :, None] * jnp.sin(phase))).astype(jnp.bfloat16)
    left_re = jnp.concatenate((weight_re, -weight_im), axis=1)
    left_im = jnp.concatenate((weight_im, weight_re), axis=1)
    return (left_re, left_im)


def general_channelize(voltages, fir_taps):
    cos_one, sin_one, twist_cos, twist_sin, cos_two, sin_two = general_tables()
    local_stations, pol_count, samples = voltages.shape
    tap_count, fft_width = fir_taps.shape
    frames = samples // fft_width - tap_count + 1
    blocks = voltages.reshape(local_stations, pol_count, frames + tap_count - 1, fft_width)
    filtered = jnp.zeros((local_stations, pol_count, frames, fft_width), jnp.float32)
    for tap_idx in range(tap_count):
        filtered = filtered + fir_taps[tap_idx] * blocks[:, :, tap_idx : tap_idx + frames].astype(
            jnp.float32
        )
    folded = filtered.astype(jnp.bfloat16).reshape(local_stations, pol_count, frames, P_SIZE, Q)
    first_table = jnp.concatenate((cos_one, -sin_one), axis=0)
    first_section = jnp.einsum(
        "spfnq,an->spfaq", folded, first_table, preferred_element_type=jnp.float32
    )
    first_re = first_section[:, :, :, :P_SIZE]
    first_im = first_section[:, :, :, P_SIZE:]
    turned = jnp.concatenate(
        (
            (first_re * twist_cos + first_im * twist_sin).astype(jnp.bfloat16),
            (first_im * twist_cos - first_re * twist_sin).astype(jnp.bfloat16),
        ),
        axis=4,
    )
    second_table = jnp.concatenate(
        (jnp.concatenate((cos_two, -sin_two), axis=1), jnp.concatenate((sin_two, cos_two), axis=1)),
        axis=0,
    )
    second = jnp.einsum("spfaq,qb->sbapf", turned, second_table, preferred_element_type=jnp.float32)
    half_q = Q // 2
    chan_re = (
        second[:, :half_q]
        .astype(jnp.bfloat16)
        .reshape(local_stations, half_q * P_SIZE, pol_count * frames)
    )
    chan_im = (
        second[:, half_q:]
        .astype(jnp.bfloat16)
        .reshape(local_stations, half_q * P_SIZE, pol_count * frames)
    )
    return jnp.stack((chan_re, chan_im), axis=0)


def combine(left_re, left_im, stacked_parts, beam_scale):
    stacked = jnp.concatenate((stacked_parts[0], stacked_parts[1]), axis=0)
    beam_re = (
        jnp.einsum("jrk,rkc->jkc", left_re, stacked, preferred_element_type=jnp.float32)
        * beam_scale
    )
    beam_im = (
        jnp.einsum("jrk,rkc->jkc", left_im, stacked, preferred_element_type=jnp.float32)
        * beam_scale
    )
    return jnp.stack((beam_re, beam_im), axis=0)


def general_device(voltages, fir_taps, delays, taper, station_map, beam_order, owners):
    stn_count = lax.axis_size("stn")
    beam_count = lax.axis_size("beam")
    stn_pos = lax.axis_index("stn")
    beam_pos = lax.axis_index("beam")
    local_stations = voltages.shape[0]
    stations = station_map.shape[0]
    group_beams = beam_order.shape[0] // beam_count
    chan_dev = CHANNELS // stn_count
    chan_ids = stn_pos * chan_dev + jnp.arange(chan_dev, dtype=jnp.int32)
    beam_scale = 1.0 / math.sqrt(P_SIZE * Q * stations)
    spectra = general_channelize(voltages, fir_taps)
    owner_model = from_root(delays, "stn", owners[beam_pos])[0]
    row_stn = jnp.arange(stn_count * local_stations, dtype=jnp.int32)
    all_rows = (
        (row_stn // local_stations * beam_count + jnp.arange(beam_count, dtype=jnp.int32)[:, None])
        * local_stations
        + row_stn % local_stations
    ).reshape(-1)
    phys_ids = station_map[all_rows]
    slot_gain = taper[beam_order[beam_pos * group_beams + jnp.arange(group_beams, dtype=jnp.int32)]]
    left_re, left_im = beam_weights(owner_model[:, phys_ids], slot_gain[:, phys_ids], chan_ids)
    full_rows = lax.all_gather(
        lax.all_to_all(spectra, "stn", split_axis=2, concat_axis=1, tiled=True),
        "beam",
        axis=1,
        tiled=True,
    )
    formed = combine(left_re, left_im, full_rows, beam_scale)
    return (formed[0], formed[1])


def on_device(voltages, fir_taps, delays, taper, station_map, beam_order, owners):
    stn_count = lax.axis_size("stn")
    beam_count = lax.axis_size("beam")
    stations = station_map.shape[0]
    chan_dev = CHANNELS // stn_count
    if (stn_count, beam_count, chan_dev) != (8, 4, P_SIZE * TILE_B):
        return general_device(
            voltages, fir_taps, delays, taper, station_map, beam_order, owners
        )
    scale = 1.0 / math.sqrt(NFFT * stations)
    data, models = exchange(voltages, fir_taps, delays[0], stn_count)
    return form_beams(data, models, taper, station_map, beam_order, owners, scale)


def solution(mesh):
    return jax.shard_map(
        on_device,
        mesh=mesh,
        in_specs=(P(("stn", "beam"), None, None), P(), P("stn", "beam", None), P(), P(), P(), P()),
        out_specs=(P("beam", "stn", None), P("beam", "stn", None)),
        check_vma=False,
    )
```

```python
import functools
import math

import jax
import jax.numpy as jnp
import numpy as np
from jax import lax
from jax.experimental import pallas as pl
from jax.experimental.pallas import tpu as pltpu
from jax.sharding import PartitionSpec as P

P_SIZE = 64
Q = 128
CHANNELS = 4096
NFFT = P_SIZE * Q
TILE_B = 8
TWO_PI = 2.0 * math.pi
PITCH = P_SIZE + 8
VMEM_LIMIT = 56 * 1024 * 1024
SEND_ORDER = (6, 1, 4, 2, 7, 3, 5)
WAIT_ORDER = (1, 2, 3, 6, 4, 7, 5)
EARLY = (((), ()), (((1, 0),), ((2, 0),)))

SIN_COEF = (6.283185272447949, -41.34169703819964, 81.60502363802586, -76.70153767014536, 42.01607576124393, -14.86832274947347, 3.199338841413777)
COS_COEF = (0.999999999885554, -19.739208743453883, 64.93938907589225, -85.45665831478402, 60.242131338256826, -26.404668186962848, 7.800131436606334, -1.4531123148805878)


def sin_cos_turns(turns):
    u = turns - jnp.round(turns)
    w = u * u
    s = jnp.full_like(u, SIN_COEF[-1])
    for coef in SIN_COEF[-2::-1]:
        s = s * w + coef
    c = jnp.full_like(u, COS_COEF[-1])
    for coef in COS_COEF[-2::-1]:
        c = c * w + coef
    return s * u, c


def dft_tables():
    first_idx, second_idx, half_idx = np.arange(P_SIZE), np.arange(Q), np.arange(Q // 2)
    first_angle = TWO_PI / P_SIZE * (first_idx[:, None] * first_idx[None, :] % P_SIZE)
    twist_angle = TWO_PI / NFFT * (first_idx[:, None] * second_idx[None, :])
    second_angle = TWO_PI / Q * (second_idx[:, None] * half_idx[None, :] % Q)
    first = np.concatenate((np.cos(first_angle), -np.sin(first_angle)), axis=0)
    cos_two = np.cos(second_angle).T.reshape(-1, TILE_B, Q)
    sin_two = np.sin(second_angle).T.reshape(-1, TILE_B, Q)
    re_rows = np.concatenate((cos_two, sin_two), axis=2)
    im_rows = np.concatenate((-sin_two, cos_two), axis=2)
    second = np.stack((re_rows, im_rows), axis=1).reshape(Q, 2 * Q)
    return (
        jnp.asarray(first.astype(np.float32).astype(jnp.bfloat16)),
        jnp.asarray(np.cos(twist_angle).astype(np.float32)),
        jnp.asarray(np.sin(twist_angle).astype(np.float32)),
        jnp.asarray(second.astype(np.float32).astype(jnp.bfloat16)),
    )


def filter_station(volt_ref, taps_ref, filt, pols, frames, tap_count):
    group = 8
    for part in range(P_SIZE // 16):
        rows = pl.ds(part * 16, 16)
        taps = [taps_ref[m, rows, :] for m in range(tap_count)]

        def body(idx, carry):
            pol, first = idx // (frames // group), idx % (frames // group) * group
            sums = [None] * group
            for step in range(group + tap_count - 1):
                value = volt_ref[pol, first + step, rows, :].astype(jnp.float32)
                for f in range(group):
                    m = step - f
                    if 0 <= m < tap_count:
                        term = taps[m] * value
                        sums[f] = term if sums[f] is None else sums[f] + term
            for f in range(group):
                filt[pol * frames + first + f, rows, :] = sums[f].astype(jnp.bfloat16)
            return carry

        lax.fori_loop(0, pols * frames // group, body, 0)


def first_section(filt, first_ref, cos_ref, sin_ref, turn_re, turn_im, count):
    table = first_ref[...]
    width = 4

    def body(idx, carry):
        c0 = idx * width
        pair = jnp.concatenate([filt[c0 + i] for i in range(width)], axis=1)
        both = jnp.dot(table, pair, preferred_element_type=jnp.float32)
        for i in range(width):
            re = both[:P_SIZE, i * Q : (i + 1) * Q]
            im = both[P_SIZE:, i * Q : (i + 1) * Q]
            rows = pl.ds(pl.multiple_of((c0 + i) * PITCH, 8), P_SIZE)
            turn_re[rows, :] = re * cos_ref[...] + im * sin_ref[...]
            turn_im[rows, :] = im * cos_ref[...] - re * sin_ref[...]
        return carry

    lax.fori_loop(0, count // width, body, 0, unroll=4)


def second_section(second_ref, turn_re, turn_im, count, store):
    table = second_ref[...]

    def body(a, carry):
        rows = pl.ds(a, count, stride=PITCH)
        turned = jnp.concatenate(
            (turn_re[rows, :].astype(jnp.bfloat16), turn_im[rows, :].astype(jnp.bfloat16)), axis=1
        )
        out = lax.dot_general(
            table, turned, (((1,), (1,)), ((), ())), preferred_element_type=jnp.float32
        )
        store(a, out.astype(jnp.bfloat16))
        return carry

    lax.fori_loop(0, P_SIZE, body, 0, unroll=8)


def exchange_kernel(
    volt_hbm,
    model_ref,
    taps_ref,
    first_ref,
    cos_ref,
    sin_ref,
    second_ref,
    data_ref,
    models_ref,
    volts,
    filt,
    turn_re,
    turn_im,
    spec_ref,
    volt_sem,
    direct_send,
    direct_recv,
    far_send,
    far_recv,
    near_send,
    near_recv,
    last_send,
    last_recv,
    model_send,
    model_recv,
    local_sem,
):
    locals_, pols, blocks = volt_hbm.shape[:3]
    tap_count = taps_ref.shape[0]
    frames = blocks - tap_count + 1
    count = pols * frames
    loads = [
        pltpu.make_async_copy(volt_hbm.at[l], volts.at[l], volt_sem.at[l]) for l in range(locals_)
    ]
    for load in loads:
        load.start()
    stn, beam = lax.axis_index("stn"), lax.axis_index("beam")
    far = (beam + 2) % 4
    near = beam + 1 - 2 * (beam % 2)

    def partner(m):
        z, x = stn // 2, stn % 2
        if m % 2:
            x = 1 - x
        if m // 2 % 2:
            z = z + 1 - 2 * (z % 2)
        if m // 4:
            z = (z + 2) % 4
        return z * 2 + x

    def row(s, b, l):
        return (s * 4 + b) * locals_ + l

    def remote(src, dst, send, recv, s, b):
        copy = pltpu.make_async_remote_copy(
            src_ref=src,
            dst_ref=dst,
            send_sem=send,
            recv_sem=recv,
            device_id=(s, b),
            device_id_type=pl.DeviceIdType.MESH,
        )
        copy.start()
        return copy

    barrier = pltpu.get_barrier_semaphore()
    peers = [(partner(m), beam) for m in range(1, 8)] + [(stn, far), (stn, near)]
    for peer in peers:
        pl.semaphore_signal(barrier, inc=1, device_id=peer, device_id_type=pl.DeviceIdType.MESH)
    pl.semaphore_wait(barrier, len(peers))

    own_copies = [pltpu.make_async_copy(model_ref, models_ref.at[stn], local_sem.at[locals_])]
    own_copies[0].start()
    direct, far_copy, near_copy, last_copy, model_copy = {}, {}, {}, {}, {}
    for m in range(1, 8):
        model_copy[m] = remote(
            model_ref, models_ref.at[stn], model_send.at[m], model_recv.at[m], partner(m), beam
        )

    def pass_on(key):
        m, l = key
        far_copy[key].wait_recv()
        place = data_ref.at[row(partner(m), far, l)]
        last_copy[key] = remote(
            place, place, last_send.at[m, l], last_recv.at[m, l], stn, near
        )

    waiting = []

    def step(key):
        m, l = key
        place = data_ref.at[row(partner(m), beam, l)]
        if m:
            direct[key].wait_recv()
            src = place
        else:
            src = spec_ref.at[stn, l]
        far_copy[key] = remote(src, place, far_send.at[m, l], far_recv.at[m, l], stn, far)
        near_copy[key] = remote(src, place, near_send.at[m, l], near_recv.at[m, l], stn, near)
        if waiting:
            pass_on(waiting.pop())
        waiting.append(key)

    for l in range(locals_):
        loads[l].wait()
        filter_station(volts.at[l], taps_ref, filt, pols, frames, tap_count)
        for key in EARLY[l][0]:
            step(key)
        first_section(filt, first_ref, cos_ref, sin_ref, turn_re, turn_im, count)
        for key in EARLY[l][1]:
            step(key)

        def store(a, value):
            spec_ref[:, l, a] = value.reshape(spec_ref.shape[0], 2 * TILE_B, count)

        second_section(second_ref, turn_re, turn_im, count, store)
        own = pltpu.make_async_copy(
            spec_ref.at[stn, l], data_ref.at[row(stn, beam, l)], local_sem.at[l]
        )
        own.start()
        own_copies.append(own)
        for m in SEND_ORDER:
            direct[m, l] = remote(
                spec_ref.at[partner(m), l],
                data_ref.at[row(stn, beam, l)],
                direct_send.at[m, l],
                direct_recv.at[m, l],
                partner(m),
                beam,
            )
        step((0, l))
    steps = [(m, l) for l in range(locals_) for m in WAIT_ORDER]
    for key in steps:
        if key not in far_copy:
            step(key)
    pass_on(waiting.pop())
    for key in far_copy:
        near_copy[key].wait_recv()
        last_copy[key].wait_recv()
        far_copy[key].wait_send()
        near_copy[key].wait_send()
        last_copy[key].wait_send()
    for copy in direct.values():
        copy.wait_send()
    for copy in model_copy.values():
        copy.wait()
    for copy in own_copies:
        copy.wait()


def exchange(voltages, fir_taps, model, stn_count):
    locals_, pols, samples = voltages.shape
    tap_count = fir_taps.shape[0]
    blocks = samples // NFFT
    count = pols * (blocks - tap_count + 1)
    stations = stn_count * 4 * locals_
    pair = pltpu.SemaphoreType.DMA((stn_count, locals_))
    one = pltpu.SemaphoreType.DMA((stn_count,))
    anywhere, vmem = pl.BlockSpec(memory_space=pl.ANY), pl.BlockSpec(memory_space=pltpu.VMEM)
    return pl.pallas_call(
        exchange_kernel,
        in_specs=[anywhere] * 2 + [vmem] * 5,
        out_specs=[anywhere] * 2,
        out_shape=[
            jax.ShapeDtypeStruct((stations, P_SIZE, 2 * TILE_B, count), jnp.bfloat16),
            jax.ShapeDtypeStruct((stn_count,) + model.shape, model.dtype),
        ],
        scratch_shapes=[
            pltpu.VMEM((locals_, pols, blocks, P_SIZE, Q), jnp.bfloat16),
            pltpu.VMEM((count, P_SIZE, Q), jnp.bfloat16),
            pltpu.VMEM((count * PITCH, Q), jnp.float32),
            pltpu.VMEM((count * PITCH, Q), jnp.float32),
            pltpu.VMEM((stn_count, locals_, P_SIZE, 2 * TILE_B, count), jnp.bfloat16),
            pltpu.SemaphoreType.DMA((locals_,)),
        ]
        + [pair] * 8
        + [one, one, pltpu.SemaphoreType.DMA((locals_ + 1,))],
        compiler_params=pltpu.CompilerParams(
            collective_id=0, has_side_effects=True, vmem_limit_bytes=VMEM_LIMIT
        ),
        name="exchange",
    )(
        voltages.reshape(locals_, pols, blocks, P_SIZE, Q),
        model,
        fir_taps.reshape(tap_count, P_SIZE, Q),
        *dft_tables(),
    )


def beam_kernel(
    step_a,
    scale,
    owners_ref,
    order_ref,
    data_ref,
    models_ref,
    taper_ref,
    map_ref,
    mask_ref,
    re_ref,
    im_ref,
    rows_ref,
    delay_ref,
    gain_ref,
    held_re,
    held_im,
):
    beams, lanes = delay_ref.shape
    stations = map_ref.shape[1]
    count = data_ref.shape[-1]
    stn, beam = lax.axis_index("stn"), lax.axis_index("beam")
    step_idx = pl.program_id(0)

    @pl.when(step_idx == 0)
    def _():
        phys = lax.broadcasted_iota(jnp.int32, (stations, stations), 0)
        pick = (phys == map_ref[...]).astype(jnp.float32).astype(jnp.bfloat16)
        station = lax.broadcasted_iota(jnp.int32, (stations, lanes), 0)
        lane_at = lax.broadcasted_iota(jnp.int32, (stations, lanes), 1)
        widen = (lane_at // (2 * TILE_B) == station).astype(jnp.float32).astype(jnp.bfloat16)

        spread = jnp.dot(pick, widen, preferred_element_type=jnp.float32).astype(jnp.bfloat16)
        for j in range(beams):
            rows_ref[pl.ds(j, 1), :] = taper_ref[pl.ds(order_ref[beam * beams + j], 1), :]
        both = jnp.concatenate((models_ref[owners_ref[beam]], rows_ref[...]), axis=0)
        high = both.astype(jnp.bfloat16)
        rest = both - high.astype(jnp.float32)
        middle = rest.astype(jnp.bfloat16)
        low = (rest - middle.astype(jnp.float32)).astype(jnp.bfloat16)
        picked = jnp.dot(
            jnp.concatenate((high, middle, low), axis=0),
            spread,
            preferred_element_type=jnp.float32,
        )
        held = picked[: 2 * beams] + picked[2 * beams : 4 * beams] + picked[4 * beams :]
        delay_ref[...] = held[:beams]
        gain_ref[...] = held[beams:]

    lane = lax.broadcasted_iota(jnp.int32, (1, lanes), 1)
    quarter = (lane // TILE_B % 2).astype(jnp.float32) * 0.25
    chan = (P_SIZE * (TILE_B * stn + lane % TILE_B) + step_idx * step_a).astype(jnp.float32)
    delay = delay_ref[...]
    sin_t, cos_t = sin_cos_turns(delay * chan * (1.0 / NFFT) - quarter)
    sin_d, cos_d = sin_cos_turns(delay * (1.0 / NFFT))
    part_re = gain_ref[...] * cos_t
    part_im = -(gain_ref[...] * sin_t)
    pitch = held_re.shape[0] // beams
    for a in range(step_a):
        if a:
            part_re, part_im = (
                part_re * cos_d + part_im * sin_d,
                part_im * cos_d - part_re * sin_d,
            )
        data = data_ref[:, a].reshape(lanes, count)
        weights = jnp.concatenate(
            [
                part.astype(jnp.bfloat16) * mask_ref[b]
                for part in (part_re, part_im)
                for b in range(TILE_B)
            ],
            axis=0,
        )
        formed = jnp.dot(weights, data, preferred_element_type=jnp.float32) * scale
        for half, out in enumerate((held_re, held_im)):
            for b in range(TILE_B):
                first = (half * TILE_B + b) * beams
                out[pl.ds(b * step_a + a, beams, stride=pitch), :] = formed[first : first + beams]
    for held, out in ((held_re, re_ref), (held_im, im_ref)):
        for j in range(beams):
            out[pl.ds(j * TILE_B, TILE_B)] = held[
                pl.ds(j * pitch, TILE_B * step_a), :
            ].reshape(TILE_B, step_a, count)


def form_beams(data, models, taper, station_map, beam_order, owners, scale):
    stations, _, tile_rows, count = data.shape
    beams = models.shape[1]
    lanes = stations * tile_rows
    step_a = 8
    mask = np.broadcast_to(
        np.arange(lanes)[None, None] % TILE_B == np.arange(TILE_B)[:, None, None],
        (TILE_B, beams, lanes),
    )
    whole = lambda x: pl.BlockSpec(x.shape, lambda i: (0,) * x.ndim)
    smem = pl.BlockSpec(memory_space=pltpu.SMEM)
    out_spec = pl.BlockSpec((beams * TILE_B, step_a, count), lambda i: (0, i, 0))
    out_shape = jax.ShapeDtypeStruct((beams * TILE_B, P_SIZE, count), jnp.float32)
    held = [models, taper, station_map[None], jnp.asarray(mask.astype(jnp.bfloat16))]
    re, im = pl.pallas_call(
        functools.partial(beam_kernel, step_a, scale),
        grid=(P_SIZE // step_a,),
        in_specs=[
            smem,
            smem,
            pl.BlockSpec((stations, step_a, tile_rows, count), lambda i: (0, i, 0, 0)),
        ]
        + [whole(x) for x in held],
        out_specs=[out_spec, out_spec],
        out_shape=[out_shape, out_shape],
        scratch_shapes=[
            pltpu.VMEM((beams, stations), jnp.float32),
            pltpu.VMEM((beams, lanes), jnp.float32),
            pltpu.VMEM((beams, lanes), jnp.float32),
            pltpu.VMEM((beams * (TILE_B + 1) * step_a, count), jnp.float32),
            pltpu.VMEM((beams * (TILE_B + 1) * step_a, count), jnp.float32),
        ],
        compiler_params=pltpu.CompilerParams(vmem_limit_bytes=VMEM_LIMIT),
        name="form_beams",
    )(owners, beam_order, data, *held)
    shape = (beams, TILE_B * P_SIZE, count)
    return re.reshape(shape), im.reshape(shape)


def from_root(value, axis, source):
    kept = jnp.where(lax.axis_index(axis) == source, value, 0).astype(value.dtype)
    return lax.psum(kept, axis)


def general_tables():
    first_idx = jnp.arange(P_SIZE, dtype=jnp.int32)
    second_idx = jnp.arange(Q, dtype=jnp.int32)
    half_idx = jnp.arange(Q // 2, dtype=jnp.int32)
    first_angle = (
        TWO_PI / P_SIZE * (first_idx[:, None] * first_idx[None, :] % P_SIZE).astype(jnp.float32)
    )
    twist_angle = (
        TWO_PI / (P_SIZE * Q) * (first_idx[:, None] * second_idx[None, :]).astype(jnp.float32)
    )
    second_angle = TWO_PI / Q * (second_idx[:, None] * half_idx[None, :] % Q).astype(jnp.float32)
    return (
        jnp.cos(first_angle).astype(jnp.bfloat16),
        jnp.sin(first_angle).astype(jnp.bfloat16),
        jnp.cos(twist_angle),
        jnp.sin(twist_angle),
        jnp.cos(second_angle).astype(jnp.bfloat16),
        jnp.sin(second_angle).astype(jnp.bfloat16),
    )


def beam_weights(delay_cols, gain_cols, chan_ids):
    phase = (
        delay_cols[:, :, None]
        * chan_ids.astype(jnp.float32)[None, None, :]
        * (TWO_PI / (P_SIZE * Q))
    )
    weight_re = (gain_cols[:, :, None] * jnp.cos(phase)).astype(jnp.bfloat16)
    weight_im = (-(gain_cols[:, :, None] * jnp.sin(phase))).astype(jnp.bfloat16)
    left_re = jnp.concatenate((weight_re, -weight_im), axis=1)
    left_im = jnp.concatenate((weight_im, weight_re), axis=1)
    return (left_re, left_im)


def general_channelize(voltages, fir_taps):
    cos_one, sin_one, twist_cos, twist_sin, cos_two, sin_two = general_tables()
    local_stations, pol_count, samples = voltages.shape
    tap_count, fft_width = fir_taps.shape
    frames = samples // fft_width - tap_count + 1
    blocks = voltages.reshape(local_stations, pol_count, frames + tap_count - 1, fft_width)
    filtered = jnp.zeros((local_stations, pol_count, frames, fft_width), jnp.float32)
    for tap_idx in range(tap_count):
        filtered = filtered + fir_taps[tap_idx] * blocks[:, :, tap_idx : tap_idx + frames].astype(
            jnp.float32
        )
    folded = filtered.astype(jnp.bfloat16).reshape(local_stations, pol_count, frames, P_SIZE, Q)
    first_table = jnp.concatenate((cos_one, -sin_one), axis=0)
    first_section = jnp.einsum(
        "spfnq,an->spfaq", folded, first_table, preferred_element_type=jnp.float32
    )
    first_re = first_section[:, :, :, :P_SIZE]
    first_im = first_section[:, :, :, P_SIZE:]
    turned = jnp.concatenate(
        (
            (first_re * twist_cos + first_im * twist_sin).astype(jnp.bfloat16),
            (first_im * twist_cos - first_re * twist_sin).astype(jnp.bfloat16),
        ),
        axis=4,
    )
    second_table = jnp.concatenate(
        (jnp.concatenate((cos_two, -sin_two), axis=1), jnp.concatenate((sin_two, cos_two), axis=1)),
        axis=0,
    )
    second = jnp.einsum("spfaq,qb->sbapf", turned, second_table, preferred_element_type=jnp.float32)
    half_q = Q // 2
    chan_re = (
        second[:, :half_q]
        .astype(jnp.bfloat16)
        .reshape(local_stations, half_q * P_SIZE, pol_count * frames)
    )
    chan_im = (
        second[:, half_q:]
        .astype(jnp.bfloat16)
        .reshape(local_stations, half_q * P_SIZE, pol_count * frames)
    )
    return jnp.stack((chan_re, chan_im), axis=0)


def combine(left_re, left_im, stacked_parts, beam_scale):
    stacked = jnp.concatenate((stacked_parts[0], stacked_parts[1]), axis=0)
    beam_re = (
        jnp.einsum("jrk,rkc->jkc", left_re, stacked, preferred_element_type=jnp.float32)
        * beam_scale
    )
    beam_im = (
        jnp.einsum("jrk,rkc->jkc", left_im, stacked, preferred_element_type=jnp.float32)
        * beam_scale
    )
    return jnp.stack((beam_re, beam_im), axis=0)


def general_device(voltages, fir_taps, delays, taper, station_map, beam_order, owners):
    stn_count = lax.axis_size("stn")
    beam_count = lax.axis_size("beam")
    stn_pos = lax.axis_index("stn")
    beam_pos = lax.axis_index("beam")
    local_stations = voltages.shape[0]
    stations = station_map.shape[0]
    group_beams = beam_order.shape[0] // beam_count
    chan_dev = CHANNELS // stn_count
    chan_ids = stn_pos * chan_dev + jnp.arange(chan_dev, dtype=jnp.int32)
    beam_scale = 1.0 / math.sqrt(P_SIZE * Q * stations)
    spectra = general_channelize(voltages, fir_taps)
    owner_model = from_root(delays, "stn", owners[beam_pos])[0]
    row_stn = jnp.arange(stn_count * local_stations, dtype=jnp.int32)
    all_rows = (
        (row_stn // local_stations * beam_count + jnp.arange(beam_count, dtype=jnp.int32)[:, None])
        * local_stations
        + row_stn % local_stations
    ).reshape(-1)
    phys_ids = station_map[all_rows]
    slot_gain = taper[beam_order[beam_pos * group_beams + jnp.arange(group_beams, dtype=jnp.int32)]]
    left_re, left_im = beam_weights(owner_model[:, phys_ids], slot_gain[:, phys_ids], chan_ids)
    full_rows = lax.all_gather(
        lax.all_to_all(spectra, "stn", split_axis=2, concat_axis=1, tiled=True),
        "beam",
        axis=1,
        tiled=True,
    )
    formed = combine(left_re, left_im, full_rows, beam_scale)
    return (formed[0], formed[1])


def on_device(voltages, fir_taps, delays, taper, station_map, beam_order, owners):
    stn_count = lax.axis_size("stn")
    beam_count = lax.axis_size("beam")
    stations = station_map.shape[0]
    chan_dev = CHANNELS // stn_count
    if (stn_count, beam_count, chan_dev) != (8, 4, P_SIZE * TILE_B):
        return general_device(
            voltages, fir_taps, delays, taper, station_map, beam_order, owners
        )
    scale = 1.0 / math.sqrt(NFFT * stations)
    data, models = exchange(voltages, fir_taps, delays[0], stn_count)
    return form_beams(data, models, taper, station_map, beam_order, owners, scale)


def solution(mesh):
    return jax.shard_map(
        on_device,
        mesh=mesh,
        in_specs=(P(("stn", "beam"), None, None), P(), P("stn", "beam", None), P(), P(), P(), P()),
        out_specs=(P("beam", "stn", None), P("beam", "stn", None)),
        check_vma=False,
    )
```

```python
import functools
import math

import jax
import jax.numpy as jnp
import numpy as np
from jax import lax
from jax.experimental import pallas as pl
from jax.experimental.pallas import tpu as pltpu
from jax.sharding import PartitionSpec as P

P_SIZE = 64
Q = 128
CHANNELS = 4096
NFFT = P_SIZE * Q
TILE_B = 8
TWO_PI = 2.0 * math.pi
PITCH = P_SIZE + 8
VMEM_LIMIT = 56 * 1024 * 1024
SEND_ORDER = (1, 6, 2, 4, 3, 7, 5)
WAIT_ORDER = (1, 2, 6, 3, 4, 7, 5)
EARLY = (((), ()), (((1, 0),), ((2, 0),)))

SIN_COEF = (6.283185272447949, -41.34169703819964, 81.60502363802586, -76.70153767014536, 42.01607576124393, -14.86832274947347, 3.199338841413777)
COS_COEF = (0.999999999885554, -19.739208743453883, 64.93938907589225, -85.45665831478402, 60.242131338256826, -26.404668186962848, 7.800131436606334, -1.4531123148805878)


def sin_cos_turns(turns):
    u = turns - jnp.round(turns)
    w = u * u
    s = jnp.full_like(u, SIN_COEF[-1])
    for coef in SIN_COEF[-2::-1]:
        s = s * w + coef
    c = jnp.full_like(u, COS_COEF[-1])
    for coef in COS_COEF[-2::-1]:
        c = c * w + coef
    return s * u, c


def dft_tables():
    first_idx, second_idx, half_idx = np.arange(P_SIZE), np.arange(Q), np.arange(Q // 2)
    first_angle = TWO_PI / P_SIZE * (first_idx[:, None] * first_idx[None, :] % P_SIZE)
    twist_angle = TWO_PI / NFFT * (first_idx[:, None] * second_idx[None, :])
    second_angle = TWO_PI / Q * (second_idx[:, None] * half_idx[None, :] % Q)
    first = np.concatenate((np.cos(first_angle), -np.sin(first_angle)), axis=0)
    cos_two = np.cos(second_angle).T.reshape(-1, TILE_B, Q)
    sin_two = np.sin(second_angle).T.reshape(-1, TILE_B, Q)
    re_rows = np.concatenate((cos_two, sin_two), axis=2)
    im_rows = np.concatenate((-sin_two, cos_two), axis=2)
    second = np.stack((re_rows, im_rows), axis=1).reshape(Q, 2 * Q)
    return (
        jnp.asarray(first.astype(np.float32).astype(jnp.bfloat16)),
        jnp.asarray(np.cos(twist_angle).astype(np.float32)),
        jnp.asarray(np.sin(twist_angle).astype(np.float32)),
        jnp.asarray(second.astype(np.float32).astype(jnp.bfloat16)),
    )


def filter_station(volt_ref, taps_ref, filt, pols, frames, tap_count):
    group = 8
    for part in range(P_SIZE // 16):
        rows = pl.ds(part * 16, 16)
        taps = [taps_ref[pl.ds(m * PITCH + part * 16, 16), :] for m in range(tap_count)]

        def body(idx, carry):
            pol, first = idx // (frames // group), idx % (frames // group) * group
            sums = [None] * group
            for step in range(group + tap_count - 1):
                value = volt_ref[pol, first + step, rows, :].astype(jnp.float32)
                for f in range(group):
                    m = step - f
                    if 0 <= m < tap_count:
                        term = taps[m] * value
                        sums[f] = term if sums[f] is None else sums[f] + term
            for f in range(group):
                filt[pol * frames + first + f, rows, :] = sums[f].astype(jnp.bfloat16)
            return carry

        lax.fori_loop(0, pols * frames // group, body, 0)


def first_section(filt, first_ref, cos_ref, sin_ref, turn_re, turn_im, count):
    table = first_ref[...]
    width = 4

    def body(idx, carry):
        c0 = idx * width
        pair = jnp.concatenate([filt[c0 + i] for i in range(width)], axis=1)
        both = jnp.dot(table, pair, preferred_element_type=jnp.float32)
        for i in range(width):
            re = both[:P_SIZE, i * Q : (i + 1) * Q]
            im = both[P_SIZE:, i * Q : (i + 1) * Q]
            rows = pl.ds(pl.multiple_of((c0 + i) * PITCH, 8), P_SIZE)
            turn_re[rows, :] = re * cos_ref[...] + im * sin_ref[...]
            turn_im[rows, :] = im * cos_ref[...] - re * sin_ref[...]
        return carry

    lax.fori_loop(0, count // width, body, 0, unroll=4)


def second_section(second_ref, turn_re, turn_im, count, store):
    table = second_ref[...]

    def body(a, carry):
        rows = pl.ds(a, count, stride=PITCH)
        turned = jnp.concatenate(
            (turn_re[rows, :].astype(jnp.bfloat16), turn_im[rows, :].astype(jnp.bfloat16)), axis=1
        )
        out = lax.dot_general(
            table, turned, (((1,), (1,)), ((), ())), preferred_element_type=jnp.float32
        )
        store(a, out.astype(jnp.bfloat16))
        return carry

    lax.fori_loop(0, P_SIZE, body, 0, unroll=8)


def exchange_kernel(
    volt_hbm,
    model_ref,
    flat_taps_ref,
    first_ref,
    cos_ref,
    sin_ref,
    second_ref,
    data_ref,
    models_ref,
    volts,
    filt,
    turn_re,
    turn_im,
    spec_ref,
    taps_ref,
    volt_sem,
    direct_send,
    direct_recv,
    far_send,
    far_recv,
    near_send,
    near_recv,
    last_send,
    last_recv,
    model_send,
    model_recv,
    local_sem,
):
    locals_, pols, blocks = volt_hbm.shape[:3]
    tap_count = flat_taps_ref.shape[0]
    frames = blocks - tap_count + 1
    count = pols * frames
    loads = [
        pltpu.make_async_copy(volt_hbm.at[l], volts.at[l], volt_sem.at[l]) for l in range(locals_)
    ]
    for load in loads:
        load.start()
    for n1 in range(P_SIZE):
        taps_ref[pl.ds(n1, tap_count, stride=PITCH), :] = flat_taps_ref[:, n1 * Q : (n1 + 1) * Q]
    stn, beam = lax.axis_index("stn"), lax.axis_index("beam")
    far = (beam + 2) % 4
    near = beam + 1 - 2 * (beam % 2)

    def partner(m):
        z, x = stn // 2, stn % 2
        if m % 2:
            x = 1 - x
        if m // 2 % 2:
            z = z + 1 - 2 * (z % 2)
        if m // 4:
            z = (z + 2) % 4
        return z * 2 + x

    def row(s, b, l):
        return (s * 4 + b) * locals_ + l

    def remote(src, dst, send, recv, s, b):
        copy = pltpu.make_async_remote_copy(
            src_ref=src,
            dst_ref=dst,
            send_sem=send,
            recv_sem=recv,
            device_id=(s, b),
            device_id_type=pl.DeviceIdType.MESH,
        )
        copy.start()
        return copy

    barrier = pltpu.get_barrier_semaphore()
    peers = [(partner(m), beam) for m in range(1, 8)] + [(stn, far), (stn, near)]
    for peer in peers:
        pl.semaphore_signal(barrier, inc=1, device_id=peer, device_id_type=pl.DeviceIdType.MESH)
    pl.semaphore_wait(barrier, len(peers))

    own_copies = [pltpu.make_async_copy(model_ref, models_ref.at[stn], local_sem.at[locals_])]
    own_copies[0].start()
    direct, far_copy, near_copy, last_copy, model_copy = {}, {}, {}, {}, {}
    for m in range(1, 8):
        model_copy[m] = remote(
            model_ref, models_ref.at[stn], model_send.at[m], model_recv.at[m], partner(m), beam
        )

    def pass_on(key):
        m, l = key
        far_copy[key].wait_recv()
        place = data_ref.at[row(partner(m), far, l)]
        last_copy[key] = remote(
            place, place, last_send.at[m, l], last_recv.at[m, l], stn, near
        )

    waiting = []

    def step(key):
        m, l = key
        place = data_ref.at[row(partner(m), beam, l)]
        if m:
            direct[key].wait_recv()
            src = place
        else:
            src = spec_ref.at[stn, l]
        far_copy[key] = remote(src, place, far_send.at[m, l], far_recv.at[m, l], stn, far)
        near_copy[key] = remote(src, place, near_send.at[m, l], near_recv.at[m, l], stn, near)
        if waiting:
            pass_on(waiting.pop())
        waiting.append(key)

    for l in range(locals_):
        loads[l].wait()
        filter_station(volts.at[l], taps_ref, filt, pols, frames, tap_count)
        for key in EARLY[l][0]:
            step(key)
        first_section(filt, first_ref, cos_ref, sin_ref, turn_re, turn_im, count)
        for key in EARLY[l][1]:
            step(key)

        def store(a, value):
            spec_ref[:, l, a] = value.reshape(spec_ref.shape[0], 2 * TILE_B, count)

        second_section(second_ref, turn_re, turn_im, count, store)
        own = pltpu.make_async_copy(
            spec_ref.at[stn, l], data_ref.at[row(stn, beam, l)], local_sem.at[l]
        )
        own.start()
        own_copies.append(own)
        for m in SEND_ORDER:
            direct[m, l] = remote(
                spec_ref.at[partner(m), l],
                data_ref.at[row(stn, beam, l)],
                direct_send.at[m, l],
                direct_recv.at[m, l],
                partner(m),
                beam,
            )
        step((0, l))
    steps = [(m, l) for l in range(locals_) for m in WAIT_ORDER]
    for key in steps:
        if key not in far_copy:
            step(key)
    pass_on(waiting.pop())
    for key in far_copy:
        near_copy[key].wait_recv()
        last_copy[key].wait_recv()
        far_copy[key].wait_send()
        near_copy[key].wait_send()
        last_copy[key].wait_send()
    for copy in direct.values():
        copy.wait_send()
    for copy in model_copy.values():
        copy.wait()
    for copy in own_copies:
        copy.wait()


def exchange(voltages, fir_taps, model, stn_count):
    locals_, pols, samples = voltages.shape
    tap_count = fir_taps.shape[0]
    blocks = samples // NFFT
    count = pols * (blocks - tap_count + 1)
    stations = stn_count * 4 * locals_
    pair = pltpu.SemaphoreType.DMA((stn_count, locals_))
    one = pltpu.SemaphoreType.DMA((stn_count,))
    anywhere, vmem = pl.BlockSpec(memory_space=pl.ANY), pl.BlockSpec(memory_space=pltpu.VMEM)
    return pl.pallas_call(
        exchange_kernel,
        in_specs=[anywhere] * 2 + [vmem] * 5,
        out_specs=[anywhere] * 2,
        out_shape=[
            jax.ShapeDtypeStruct((stations, P_SIZE, 2 * TILE_B, count), jnp.bfloat16),
            jax.ShapeDtypeStruct((stn_count,) + model.shape, model.dtype),
        ],
        scratch_shapes=[
            pltpu.VMEM((locals_, pols, blocks, P_SIZE, Q), jnp.bfloat16),
            pltpu.VMEM((count, P_SIZE, Q), jnp.bfloat16),
            pltpu.VMEM((count * PITCH, Q), jnp.float32),
            pltpu.VMEM((count * PITCH, Q), jnp.float32),
            pltpu.VMEM((stn_count, locals_, P_SIZE, 2 * TILE_B, count), jnp.bfloat16),
            pltpu.VMEM((tap_count * PITCH, Q), jnp.float32),
            pltpu.SemaphoreType.DMA((locals_,)),
        ]
        + [pair] * 8
        + [one, one, pltpu.SemaphoreType.DMA((locals_ + 1,))],
        compiler_params=pltpu.CompilerParams(
            collective_id=0, has_side_effects=True, vmem_limit_bytes=VMEM_LIMIT
        ),
        name="exchange",
    )(
        voltages.reshape(locals_, pols, blocks, P_SIZE, Q),
        model,
        fir_taps,
        *dft_tables(),
    )


def beam_kernel(
    step_a,
    scale,
    owners_ref,
    order_ref,
    data_ref,
    models_ref,
    taper_ref,
    map_ref,
    mask_ref,
    re_ref,
    im_ref,
    rows_ref,
    delay_ref,
    gain_ref,
    held_re,
    held_im,
):
    beams, lanes = delay_ref.shape
    stations = map_ref.shape[1]
    count = data_ref.shape[-1]
    stn, beam = lax.axis_index("stn"), lax.axis_index("beam")
    step_idx = pl.program_id(0)

    @pl.when(step_idx == 0)
    def _():
        phys = lax.broadcasted_iota(jnp.int32, (stations, stations), 0)
        pick = (phys == map_ref[...]).astype(jnp.float32).astype(jnp.bfloat16)
        station = lax.broadcasted_iota(jnp.int32, (stations, lanes), 0)
        lane_at = lax.broadcasted_iota(jnp.int32, (stations, lanes), 1)
        widen = (lane_at // (2 * TILE_B) == station).astype(jnp.float32).astype(jnp.bfloat16)

        spread = jnp.dot(pick, widen, preferred_element_type=jnp.float32).astype(jnp.bfloat16)
        for j in range(beams):
            rows_ref[pl.ds(j, 1), :] = taper_ref[pl.ds(order_ref[beam * beams + j], 1), :]
        both = jnp.concatenate((models_ref[owners_ref[beam]], rows_ref[...]), axis=0)
        high = both.astype(jnp.bfloat16)
        rest = both - high.astype(jnp.float32)
        middle = rest.astype(jnp.bfloat16)
        low = (rest - middle.astype(jnp.float32)).astype(jnp.bfloat16)
        picked = jnp.dot(
            jnp.concatenate((high, middle, low), axis=0),
            spread,
            preferred_element_type=jnp.float32,
        )
        held = picked[: 2 * beams] + picked[2 * beams : 4 * beams] + picked[4 * beams :]
        delay_ref[...] = held[:beams]
        gain_ref[...] = held[beams:]

    lane = lax.broadcasted_iota(jnp.int32, (1, lanes), 1)
    quarter = (lane // TILE_B % 2).astype(jnp.float32) * 0.25
    chan = (P_SIZE * (TILE_B * stn + lane % TILE_B) + step_idx * step_a).astype(jnp.float32)
    delay = delay_ref[...]
    sin_t, cos_t = sin_cos_turns(delay * chan * (1.0 / NFFT) - quarter)
    sin_d, cos_d = sin_cos_turns(delay * (1.0 / NFFT))
    part_re = gain_ref[...] * cos_t
    part_im = -(gain_ref[...] * sin_t)
    pitch = held_re.shape[0] // beams
    for a in range(step_a):
        if a:
            part_re, part_im = (
                part_re * cos_d + part_im * sin_d,
                part_im * cos_d - part_re * sin_d,
            )
        data = data_ref[:, a].reshape(lanes, count)
        weights = jnp.concatenate(
            [
                part.astype(jnp.bfloat16) * mask_ref[b]
                for part in (part_re, part_im)
                for b in range(TILE_B)
            ],
            axis=0,
        )
        formed = jnp.dot(weights, data, preferred_element_type=jnp.float32) * scale
        for half, out in enumerate((held_re, held_im)):
            for b in range(TILE_B):
                first = (half * TILE_B + b) * beams
                out[pl.ds(b * step_a + a, beams, stride=pitch), :] = formed[first : first + beams]
    for held, out in ((held_re, re_ref), (held_im, im_ref)):
        for j in range(beams):
            out[pl.ds(j * TILE_B, TILE_B)] = held[
                pl.ds(j * pitch, TILE_B * step_a), :
            ].reshape(TILE_B, step_a, count)


def form_beams(data, models, taper, station_map, beam_order, owners, scale):
    stations, _, tile_rows, count = data.shape
    beams = models.shape[1]
    lanes = stations * tile_rows
    step_a = 8
    mask = np.broadcast_to(
        np.arange(lanes)[None, None] % TILE_B == np.arange(TILE_B)[:, None, None],
        (TILE_B, beams, lanes),
    )
    whole = lambda x: pl.BlockSpec(x.shape, lambda i: (0,) * x.ndim)
    smem = pl.BlockSpec(memory_space=pltpu.SMEM)
    out_spec = pl.BlockSpec((beams * TILE_B, step_a, count), lambda i: (0, i, 0))
    out_shape = jax.ShapeDtypeStruct((beams * TILE_B, P_SIZE, count), jnp.float32)
    held = [models, taper, station_map[None], jnp.asarray(mask.astype(jnp.bfloat16))]
    re, im = pl.pallas_call(
        functools.partial(beam_kernel, step_a, scale),
        grid=(P_SIZE // step_a,),
        in_specs=[
            smem,
            smem,
            pl.BlockSpec((stations, step_a, tile_rows, count), lambda i: (0, i, 0, 0)),
        ]
        + [whole(x) for x in held],
        out_specs=[out_spec, out_spec],
        out_shape=[out_shape, out_shape],
        scratch_shapes=[
            pltpu.VMEM((beams, stations), jnp.float32),
            pltpu.VMEM((beams, lanes), jnp.float32),
            pltpu.VMEM((beams, lanes), jnp.float32),
            pltpu.VMEM((beams * (TILE_B + 1) * step_a, count), jnp.float32),
            pltpu.VMEM((beams * (TILE_B + 1) * step_a, count), jnp.float32),
        ],
        compiler_params=pltpu.CompilerParams(vmem_limit_bytes=VMEM_LIMIT),
        name="form_beams",
    )(owners, beam_order, data, *held)
    shape = (beams, TILE_B * P_SIZE, count)
    return re.reshape(shape), im.reshape(shape)


def from_root(value, axis, source):
    kept = jnp.where(lax.axis_index(axis) == source, value, 0).astype(value.dtype)
    return lax.psum(kept, axis)


def general_tables():
    first_idx = jnp.arange(P_SIZE, dtype=jnp.int32)
    second_idx = jnp.arange(Q, dtype=jnp.int32)
    half_idx = jnp.arange(Q // 2, dtype=jnp.int32)
    first_angle = (
        TWO_PI / P_SIZE * (first_idx[:, None] * first_idx[None, :] % P_SIZE).astype(jnp.float32)
    )
    twist_angle = (
        TWO_PI / (P_SIZE * Q) * (first_idx[:, None] * second_idx[None, :]).astype(jnp.float32)
    )
    second_angle = TWO_PI / Q * (second_idx[:, None] * half_idx[None, :] % Q).astype(jnp.float32)
    return (
        jnp.cos(first_angle).astype(jnp.bfloat16),
        jnp.sin(first_angle).astype(jnp.bfloat16),
        jnp.cos(twist_angle),
        jnp.sin(twist_angle),
        jnp.cos(second_angle).astype(jnp.bfloat16),
        jnp.sin(second_angle).astype(jnp.bfloat16),
    )


def beam_weights(delay_cols, gain_cols, chan_ids):
    phase = (
        delay_cols[:, :, None]
        * chan_ids.astype(jnp.float32)[None, None, :]
        * (TWO_PI / (P_SIZE * Q))
    )
    weight_re = (gain_cols[:, :, None] * jnp.cos(phase)).astype(jnp.bfloat16)
    weight_im = (-(gain_cols[:, :, None] * jnp.sin(phase))).astype(jnp.bfloat16)
    left_re = jnp.concatenate((weight_re, -weight_im), axis=1)
    left_im = jnp.concatenate((weight_im, weight_re), axis=1)
    return (left_re, left_im)


def general_channelize(voltages, fir_taps):
    cos_one, sin_one, twist_cos, twist_sin, cos_two, sin_two = general_tables()
    local_stations, pol_count, samples = voltages.shape
    tap_count, fft_width = fir_taps.shape
    frames = samples // fft_width - tap_count + 1
    blocks = voltages.reshape(local_stations, pol_count, frames + tap_count - 1, fft_width)
    filtered = jnp.zeros((local_stations, pol_count, frames, fft_width), jnp.float32)
    for tap_idx in range(tap_count):
        filtered = filtered + fir_taps[tap_idx] * blocks[:, :, tap_idx : tap_idx + frames].astype(
            jnp.float32
        )
    folded = filtered.astype(jnp.bfloat16).reshape(local_stations, pol_count, frames, P_SIZE, Q)
    first_table = jnp.concatenate((cos_one, -sin_one), axis=0)
    first_section = jnp.einsum(
        "spfnq,an->spfaq", folded, first_table, preferred_element_type=jnp.float32
    )
    first_re = first_section[:, :, :, :P_SIZE]
    first_im = first_section[:, :, :, P_SIZE:]
    turned = jnp.concatenate(
        (
            (first_re * twist_cos + first_im * twist_sin).astype(jnp.bfloat16),
            (first_im * twist_cos - first_re * twist_sin).astype(jnp.bfloat16),
        ),
        axis=4,
    )
    second_table = jnp.concatenate(
        (jnp.concatenate((cos_two, -sin_two), axis=1), jnp.concatenate((sin_two, cos_two), axis=1)),
        axis=0,
    )
    second = jnp.einsum("spfaq,qb->sbapf", turned, second_table, preferred_element_type=jnp.float32)
    half_q = Q // 2
    chan_re = (
        second[:, :half_q]
        .astype(jnp.bfloat16)
        .reshape(local_stations, half_q * P_SIZE, pol_count * frames)
    )
    chan_im = (
        second[:, half_q:]
        .astype(jnp.bfloat16)
        .reshape(local_stations, half_q * P_SIZE, pol_count * frames)
    )
    return jnp.stack((chan_re, chan_im), axis=0)


def combine(left_re, left_im, stacked_parts, beam_scale):
    stacked = jnp.concatenate((stacked_parts[0], stacked_parts[1]), axis=0)
    beam_re = (
        jnp.einsum("jrk,rkc->jkc", left_re, stacked, preferred_element_type=jnp.float32)
        * beam_scale
    )
    beam_im = (
        jnp.einsum("jrk,rkc->jkc", left_im, stacked, preferred_element_type=jnp.float32)
        * beam_scale
    )
    return jnp.stack((beam_re, beam_im), axis=0)


def general_device(voltages, fir_taps, delays, taper, station_map, beam_order, owners):
    stn_count = lax.axis_size("stn")
    beam_count = lax.axis_size("beam")
    stn_pos = lax.axis_index("stn")
    beam_pos = lax.axis_index("beam")
    local_stations = voltages.shape[0]
    stations = station_map.shape[0]
    group_beams = beam_order.shape[0] // beam_count
    chan_dev = CHANNELS // stn_count
    chan_ids = stn_pos * chan_dev + jnp.arange(chan_dev, dtype=jnp.int32)
    beam_scale = 1.0 / math.sqrt(P_SIZE * Q * stations)
    spectra = general_channelize(voltages, fir_taps)
    owner_model = from_root(delays, "stn", owners[beam_pos])[0]
    row_stn = jnp.arange(stn_count * local_stations, dtype=jnp.int32)
    all_rows = (
        (row_stn // local_stations * beam_count + jnp.arange(beam_count, dtype=jnp.int32)[:, None])
        * local_stations
        + row_stn % local_stations
    ).reshape(-1)
    phys_ids = station_map[all_rows]
    slot_gain = taper[beam_order[beam_pos * group_beams + jnp.arange(group_beams, dtype=jnp.int32)]]
    left_re, left_im = beam_weights(owner_model[:, phys_ids], slot_gain[:, phys_ids], chan_ids)
    full_rows = lax.all_gather(
        lax.all_to_all(spectra, "stn", split_axis=2, concat_axis=1, tiled=True),
        "beam",
        axis=1,
        tiled=True,
    )
    formed = combine(left_re, left_im, full_rows, beam_scale)
    return (formed[0], formed[1])


def on_device(voltages, fir_taps, delays, taper, station_map, beam_order, owners):
    stn_count = lax.axis_size("stn")
    beam_count = lax.axis_size("beam")
    stations = station_map.shape[0]
    chan_dev = CHANNELS // stn_count
    if (stn_count, beam_count, chan_dev) != (8, 4, P_SIZE * TILE_B):
        return general_device(
            voltages, fir_taps, delays, taper, station_map, beam_order, owners
        )
    scale = 1.0 / math.sqrt(NFFT * stations)
    data, models = exchange(voltages, fir_taps, delays[0], stn_count)
    return form_beams(data, models, taper, station_map, beam_order, owners, scale)


def solution(mesh):
    return jax.shard_map(
        on_device,
        mesh=mesh,
        in_specs=(P(("stn", "beam"), None, None), P(), P("stn", "beam", None), P(), P(), P(), P()),
        out_specs=(P("beam", "stn", None), P("beam", "stn", None)),
        check_vma=False,
    )
```
